512 devices in a mesh: patch: 64 (over z_lo, y, core), tp: 8 (over z_hi, x).
Axes of the slice: x: 4, y: 8, z: 8 (z_hi: 2, z_lo: 4; z = z_hi * 4 + z_lo), core: 2. Of those that a mesh axis runs over, the one named last changes fastest.
Arguments:
- queries: bfloat16 [2, 2048, 2048], P(None, 'patch', 'tp'), may hold values from -8 to 8
- new_keys: bfloat16 [2, 2048, 2048], P(None, 'patch', 'tp'), may hold values from -4 to 4
- new_values: bfloat16 [2, 2048, 2048], P(None, 'patch', 'tp'), may hold values from -6 to 6
- prev_keys: bfloat16 [2048, 2048], P('patch', 'tp'), may hold values from -4 to 4
- prev_values: bfloat16 [2048, 2048], P('patch', 'tp'), may hold values from -6 to 6
- kv_basis: bfloat16 [2, 16, 128, 32], P(None, 'tp'), may hold values from -0.5 to 0.5
- out_weight: bfloat16 [2048, 3072], P('tp'), may hold values from -0.1875 to 0.1875
- out_gate: float32 [2, 3072], P(None, 'tp'), may hold values from 0.5 to 1.5
Outputs:
- block_output: bfloat16 [2, 2048, 3072], P(None, 'patch', 'tp')
The draws below stay inside these ranges and needn't reach their ends.
All inputs are finite; a program needn't handle non-finite values.
Results may differ from the reference program's by a relative error of at most 0.018.
The reference program's roundings to bfloat16 on the way (of `shared_keys`, `coefficients`, `weights` and `attended`) count: a program that leaves them out, or rounds other values in their place, can miss the bound.
Values may be sent and summed in bfloat16 or wider, within the bound.
A program may use at most 64 MiB of HBM per device.

```python
import math
import jax
import jax.numpy as jnp
from jax import lax

D = 3072
HD = 128
HEADS = 16
RANK = 32
STEPS = 2
TOKENS = 2048


def draw_queries(key, part):
    key = jax.random.fold_in(key, 11)
    full_shape = (STEPS, TOKENS, HEADS * HD)
    values = jnp.clip(3.0 * jax.random.normal(key, full_shape, jnp.float32), -8.0, 8.0)
    return values.astype(jnp.bfloat16)


def draw_prev_keys(key, part):
    key = jax.random.fold_in(key, 12)
    full_shape = (TOKENS, HEADS * HD)
    key_field = jnp.clip(jax.random.normal(key, full_shape, jnp.float32), -4.0, 4.0)
    return key_field.astype(jnp.bfloat16)


def draw_new_keys(key, part):
    key = jax.random.fold_in(key, 13)
    full_shape = (STEPS, TOKENS, HEADS * HD)
    key_field = jnp.clip(jax.random.normal(key, full_shape, jnp.float32), -4.0, 4.0)
    return key_field.astype(jnp.bfloat16)


def with_spikes(values, rng, source, target, shards_of, factor):
    owner, partner = [(jnp.arange(values.shape[position]) // (values.shape[position] // shards_of)).reshape([-1 if axis == position else 1 for axis in range(values.ndim)]) for position in (source, target)]
    chosen = jax.random.permutation(rng, shards_of)[partner]
    strong = (owner == chosen) | (owner == (partner + shards_of // 2) % shards_of)
    return jnp.where(strong, factor * values, values)


def levels(rng, shape, cuts, smallest, top_value):
    gain, own = 1.0, jax.random.fold_in(rng, 6)
    for dim, parts in cuts:
        steps = jnp.exp(jax.random.uniform(jax.random.fold_in(own, dim), (parts,), jnp.float32, smallest / len(cuts), top_value / len(cuts)))
        gain = gain * jnp.repeat(steps, shape[dim] // parts).reshape([-1 if axis == dim else 1 for axis in range(len(shape))])
    return gain


def bell_draw(key, dims, width, most, pieces=(), held_as=jnp.bfloat16):
    values = width * jax.random.normal(key, dims, jnp.float32)
    if pieces:
        values = values * levels(key, dims, pieces, -0.22, 0.18)
    return jnp.clip(values, -most, most).astype(held_as)


def bell_draw_with(stream_key, extent, spread, most, split, heavy, dtype=jnp.bfloat16):
    values = spread * jax.random.normal(stream_key, extent, jnp.float32)
    if split:
        values = values * levels(stream_key, extent, split, -0.22, 0.18)
    return jnp.clip(with_spikes(values, jax.random.fold_in(stream_key, 3), *heavy), -most, most).astype(dtype)


def setup_inputs(seed: int = 0) -> dict:
    key_list = jax.random.split(jax.random.key(seed), 9)
    queries = draw_queries(jax.random.fold_in(key_list[8], 71), 0)
    new_keys = draw_new_keys(jax.random.fold_in(key_list[8], 71), 0)
    new_values = bell_draw(key_list[2], (STEPS, TOKENS, HEADS * HD), 1.0, 6.0, ((1, 64), (2, 8)))
    prev_keys = draw_prev_keys(jax.random.fold_in(key_list[8], 71), 0)
    prev_values = bell_draw(key_list[4], (TOKENS, HEADS * HD), 1.0, 6.0, ((0, 64), (1, 8)))
    kv_basis = bell_draw(key_list[5], (2, HEADS, HD, RANK), HD ** -0.5, 0.5, ((1, 8),))
    out_weight = bell_draw_with(key_list[6], (HEADS * HD, D), (HEADS * HD) ** -0.5, 0.1875, ((0, 8),), (0, 1, 8, 2.0))
    out_gate = jnp.clip(0.5 + 1.0 * jax.random.uniform(key_list[7], (STEPS, D), jnp.float32) ** levels(key_list[7], (STEPS, D), ((1, 8),), -0.2, 0.2), 0.5, 1.5)
    return {"queries": queries, "new_keys": new_keys, "new_values": new_values, "prev_keys": prev_keys, "prev_values": prev_values, "kv_basis": kv_basis, "out_weight": out_weight, "out_gate": out_gate}


def update(shared, fresh_rows, basis_one):
    residual = (fresh_rows.astype(jnp.float32) - shared.astype(jnp.float32)).reshape(TOKENS, HEADS, HD)
    coefficients = jnp.einsum("thd,hdr->thr", residual, basis_one.astype(jnp.float32), precision=lax.Precision.HIGHEST).astype(jnp.bfloat16)
    low_rank = jnp.einsum("thr,hdr->thd", coefficients.astype(jnp.float32), basis_one.astype(jnp.float32), precision=lax.Precision.HIGHEST)
    rebuilt = shared.astype(jnp.float32).reshape(TOKENS, HEADS, HD) + low_rank
    return rebuilt.astype(jnp.bfloat16).reshape(TOKENS, HEADS * HD)


def by_head(array):
    return array.reshape(TOKENS, HEADS, HD).transpose(1, 0, 2)


def attend(queries_now, shared_keys, shared_values):
    score_scale = HD ** -0.5
    block_size = math.gcd(TOKENS, 1024)

    def per_head(operands):
        queries_head, keys_head, values_head = operands

        def one_block(queries_block):
            scores = jnp.einsum("qd,kd->qk", queries_block.astype(jnp.float32), keys_head.astype(jnp.float32), precision=lax.Precision.HIGHEST) * score_scale
            row_max = jnp.max(scores, axis=1, keepdims=True)
            exponent = jnp.exp(scores - row_max)
            row_total = jnp.sum(exponent, axis=1, keepdims=True)
            weights = exponent.astype(jnp.bfloat16)
            summed = jnp.einsum("qk,kd->qd", weights.astype(jnp.float32), values_head.astype(jnp.float32), precision=lax.Precision.HIGHEST)
            return (summed / row_total).astype(jnp.bfloat16)

        blocks = queries_head.reshape(TOKENS // block_size, block_size, HD)
        return lax.map(one_block, blocks).reshape(TOKENS, HD)

    result = lax.map(per_head, (by_head(queries_now), by_head(shared_keys), by_head(shared_values)))
    return result.transpose(1, 0, 2).reshape(TOKENS, HEADS * HD)


def reference(queries, new_keys, new_values, prev_keys, prev_values, kv_basis, out_weight, out_gate):
    shared_keys = prev_keys
    shared_values = prev_values
    results = []
    for number in range(STEPS):
        shared_keys = update(shared_keys, new_keys[number], kv_basis[0])
        shared_values = update(shared_values, new_values[number], kv_basis[1])
        attended = attend(queries[number], shared_keys, shared_values)
        projected = jnp.dot(attended, out_weight, preferred_element_type=jnp.float32)
        results.append((out_gate[number][None, :] * projected).astype(jnp.bfloat16))
    return jnp.stack(results)
```

```python
import functools

import jax
import jax.numpy as jnp
from jax import lax
from jax.experimental import pallas as pl
from jax.experimental.pallas import tpu as pltpu
from jax.sharding import PartitionSpec as P

MESH = pl.DeviceIdType.MESH
NZ = 4
NY = 8
NX = 4
HD = 128
CHUNKS = 4
PER = NZ // CHUNKS
HALF = NY // 2


def slot_of(way, distance):
    if distance == 0 or distance == HALF:
        return 2 * distance - (distance == HALF)
    return 2 * distance - 1 + way


def far_way(chunk):
    return 0 if chunk < CHUNKS // 2 else 1


def nt_dot(a, b):
    return lax.dot_general(a, b, (((1,), (1,)), ((), ())), preferred_element_type=jnp.float32)


def nn_dot(a, b):
    return jnp.dot(a, b, preferred_element_type=jnp.float32)


def kernel(
    q_hbm, nk_hbm, nv_hbm, pk_hbm, pv_hbm, basis_hbm, w_hbm, out_ref,
    q_ref, nk_ref, nv_ref, pk_ref, pv_ref, basis_ref, w_ref,
    zsend, kv, qbuf, scores, weights, asend, abuf, hsend, hrecv,
    in_sem, zs_sem, zr_sem, qs_sem, qr_sem, rs_sem, rr_sem, cs_sem, cr_sem,
    fs_sem, fr_sem, as_sem, ar_sem, ws_sem, wr_sem, vs_sem, vr_sem, hs_sem, hr_sem,
):
    rows = pk_ref.shape[0]
    columns = out_ref.shape[2]
    patch, tp = lax.axis_index("patch"), lax.axis_index("tp")
    core = patch % 2
    y = (patch // 2) % NY
    z = patch // (2 * NY)
    x = tp % NX
    zh = tp // NX

    def at(z_to=None, y_to=None, core_to=None, x_to=None, zh_to=None):
        z_t = z if z_to is None else z_to
        y_t = y if y_to is None else y_to
        c_t = core if core_to is None else core_to
        x_t = x if x_to is None else x_to
        h_t = zh if zh_to is None else zh_to
        return ((z_t * NY + y_t) * 2 + c_t, h_t * NX + x_t)

    z_peers = [lax.rem(z + k, NZ) for k in range(NZ)]
    z_back = [lax.rem(z + NZ - k, NZ) for k in range(NZ)]
    x_peers = [lax.rem(x + k, NX) for k in range(NX)]
    x_back = [lax.rem(x + NX - k, NX) for k in range(NX)]
    y_next = [lax.rem(y + 1, NY), lax.rem(y + NY - 1, NY)]
    y_after = [lax.rem(y + 2, NY), lax.rem(y + NY - 2, NY)]

    halves = (1 - zh, zh)
    w_rows = w_hbm.shape[0]
    core_rows = pl.ds(pl.multiple_of(core * (w_rows // 2), w_rows // 2), w_rows // 2)

    def columns_of(which, x_to):
        return pl.ds(pl.multiple_of((halves[which] * NX + x_to) * columns, columns), columns)

    fetches = [
        pltpu.make_async_copy(source, target, in_sem.at[number])
        for number, (source, target) in enumerate(
            (
                (basis_hbm, basis_ref), (nk_hbm, nk_ref), (pk_hbm, pk_ref), (nv_hbm, nv_ref),
                (pv_hbm, pv_ref), (q_hbm, q_ref),
                (w_hbm.at[:, columns_of(0, x)], w_ref.at[0, x]), (w_hbm.at[:, columns_of(1, x)], w_ref.at[1, x]),
            )
        )
    ]
    for fetch in fetches:
        fetch.start()

    barrier = pltpu.get_barrier_semaphore()
    others = [(k, j) for k in range(NZ) for j in range(NX) if k or j]
    friends = [at(z_to=z_peers[k], x_to=x_peers[j]) for k, j in others]
    friends += [at(y_to=y_next[way]) for way in range(2)]
    friends += [at(y_to=y_after[way], core_to=c) for way in range(2) for c in (core, 1 - core)]
    friends += [at(core_to=1 - core), at(zh_to=1 - zh)]
    for friend in friends:
        pl.semaphore_signal(barrier, inc=1, device_id=friend, device_id_type=MESH)

    for fetch in fetches[:6]:
        fetch.wait()
    chains = [(member, head) for member in range(2) for head in range(2)]
    fresh_refs, prev_refs = (nk_ref, nv_ref), (pk_ref, pv_ref)
    columns_of_head = [slice(head * HD, (head + 1) * HD) for head in range(2)]
    basis = {(member, head): basis_ref[member, head] for member, head in chains}
    shared, mapped, shared_mapped = {}, {}, {}
    for member, head in chains:
        cols = columns_of_head[head]
        shared[member, head] = prev_refs[member][:, cols]
        fresh = fresh_refs[member]
        stacked = jnp.concatenate([fresh[0, :, cols], fresh[1, :, cols], shared[member, head]], axis=0)
        mapped[member, head] = nt_dot(stacked, basis[member, head])
        shared_mapped[member, head] = mapped[member, head][2 * rows :]
    for step in range(2):
        low_rank = {}
        for chain in chains:
            coefficients = mapped[chain][step * rows : (step + 1) * rows] - shared_mapped[chain]
            low_rank[chain] = nn_dot(coefficients.astype(jnp.bfloat16), basis[chain])
        for chain in chains:
            shared[chain] = (shared[chain].astype(jnp.float32) + low_rank[chain]).astype(jnp.bfloat16)
            if step == 0:
                shared_mapped[chain] = nt_dot(shared[chain], basis[chain])
        for member, head in chains:
            zsend[2 * head + step, member] = shared[member, head]
    for head in range(2):
        for step in range(2):
            zsend[2 * head + step, 2] = q_ref[step, :, head * HD : (head + 1) * HD]


    pl.semaphore_wait(barrier, len(friends))

    started = []

    def send(src, dst, send_sem, recv_sem, device):
        copy = pltpu.make_async_remote_copy(
            src_ref=src, dst_ref=dst, send_sem=send_sem, recv_sem=recv_sem, device_id=device, device_id_type=MESH
        )
        copy.start()
        started.append(copy)
        return copy

    z_copies, q_copies = {}, {}
    for k in range(1, NZ):
        z_copies[k] = send(
            zsend.at[z_peers[k], pl.ds(0, 2)], kv.at[0, 0, k], zs_sem.at[k], zr_sem.at[k], at(z_to=z_peers[k])
        )
    w_copies = {}
    for k in (2, 1, 3):
        for which in range(2):
            w_copies[k, which] = send(
                w_hbm.at[core_rows, columns_of(which, x_peers[k])], w_ref.at[which, x, core_rows],
                ws_sem.at[k, which], wr_sem.at[k, which], at(x_to=x_peers[k]),
            )
    kv[0, 0, 0] = zsend[z, 0:2]
    qbuf[0] = zsend[z, 2]

    ring, share, far_other = {}, {}, {}

    def push(way, distance, chunk, step):
        piece = pl.ds(chunk * PER, PER)
        ring[way, distance + step, chunk] = send(
            kv.at[0, slot_of(way, distance), piece],
            kv.at[0, slot_of(way, distance + step), piece],
            rs_sem.at[way, distance + step - 1, chunk],
            rr_sem.at[way, distance + step - 1, chunk],
            at(y_to=(y_next if step == 1 else y_after)[way]),
        )

    def far_push(way, chunk):
        push(way, HALF - 2, chunk, 2)
        piece = pl.ds(chunk * PER, PER)
        far_other[chunk] = send(
            kv.at[0, slot_of(way, HALF - 2), piece], kv.at[1, slot_of(0, HALF), piece],
            fs_sem.at[chunk], fr_sem.at[chunk], at(y_to=y_after[way], core_to=1 - core),
        )

    def share_core(way, distance, chunk):
        parts = 1 if distance < HALF - 1 else 2
        count = CHUNKS // parts
        if (chunk + 1) % count:
            return
        part = chunk // count
        piece = pl.ds(part * count * PER, count * PER)
        slot = slot_of(way, distance)
        share[slot, part] = send(
            kv.at[0, slot, piece],
            kv.at[1, slot, piece],
            cs_sem.at[slot, part],
            cr_sem.at[slot, part],
            at(core_to=1 - core),
        )

    lag = 2
    for chunk in range(CHUNKS + lag):
        if chunk < CHUNKS:
            for k in range(chunk * PER, (chunk + 1) * PER):
                if k:
                    z_copies[k].wait_recv()
            for way in range(2):
                push(way, 0, chunk, 2)
            share_core(0, 0, chunk)
        if chunk >= lag:
            for way in range(2):
                push(way, 0, chunk - lag, 1)
        if chunk == 0:
            for k in range(1, NZ):
                q_copies[k] = send(
                    zsend.at[z_peers[k], 2], qbuf.at[k], qs_sem.at[k], qr_sem.at[k], at(z_to=z_peers[k])
                )
    for k in range(1, NZ):
        q_copies[k].wait_recv()
    queries = qbuf[...].reshape(NZ * rows, HD)
    scale = HD ** (-0.5)
    block = NZ * rows
    lane_max = []

    def score(side, distance):
        first, last = slot_of(0, distance), slot_of(1, distance)
        count = last - first + 1
        keys = kv[side, first : last + 1, :, 0].reshape(count * block, HD)
        begin = (side * NY + first) * block
        found = nt_dot(queries, keys) * scale
        scores[:, begin : begin + count * block] = found
        for number in range(count):
            piece = found[:, number * block : (number + 1) * block]
            lane_max[:] = [jnp.maximum(lane_max[0], piece) if lane_max else piece]

    def score_other(distance):
        for slot in sorted({slot_of(0, distance), slot_of(1, distance)}):
            for part in range(2):
                if (slot, part) in share:
                    share[slot, part].wait_recv()
        for chunk in range(CHUNKS if distance == HALF else 0):
            far_other[chunk].wait_recv()
        score(1, distance)

    score(0, 0)
    for chunk in range(CHUNKS):
        for way in range(2):
            ring[way, HALF - 2, chunk].wait_recv()
            push(way, HALF - 2, chunk, 1)
        far_push(far_way(chunk), chunk)
        for way in range(2):
            share_core(way, HALF - 2, chunk)
    for chunk in range(CHUNKS):
        for way in range(2):
            ring[way, 1, chunk].wait_recv()
            share_core(way, 1, chunk)
    score(0, 2)
    score(0, 1)
    score_other(0)
    for chunk in range(CHUNKS):
        for way in range(2):
            ring[way, HALF - 1, chunk].wait_recv()
            share_core(way, HALF - 1, chunk)
    score_other(2)
    score_other(1)
    score(0, HALF - 1)
    for chunk in range(CHUNKS):
        ring[far_way(chunk), HALF, chunk].wait_recv()
    score(0, HALF)
    score_other(HALF)
    score_other(HALF - 1)

    row_max = jnp.max(lane_max[0], axis=1, keepdims=True)
    lane_total = jnp.zeros((block, block), jnp.float32)
    side_keys = NY * block
    summed = jnp.zeros((block, HD), jnp.float32)
    for side in range(2):
        for index in range(side * NY, (side + 1) * NY):
            span = slice(index * block, (index + 1) * block)
            exponent = jnp.exp(scores[:, span] - row_max)
            lane_total = lane_total + exponent
            weights[:, span] = exponent.astype(jnp.bfloat16)
        values = kv[side, :, :, 1].reshape(side_keys, HD)
        summed += nn_dot(weights[:, side * side_keys : (side + 1) * side_keys], values)
    row_total = jnp.sum(lane_total, axis=1, keepdims=True)
    attended = (summed / row_total).astype(jnp.bfloat16)
    asend[...] = attended.reshape(NZ, rows, HD)

    earlier = list(started)
    a_copies = {}
    for j in (2, 1, 3, 0):
        for k in (2, 1, 3, 0):
            if k or j:
                a_copies[k, j] = send(
                    asend.at[k], abuf.at[x, z], as_sem.at[k, j], ar_sem.at[k, j], at(z_to=z_back[k], x_to=x_peers[j])
                )
    abuf[x, z] = asend[0]

    v_copies = {}
    for which in range(2):
        for k in (1, 3, 2):
            w_copies[k, which].wait_recv()
            there = w_ref.at[which, x_back[k], core_rows]
            v_copies[k, which] = send(there, there, vs_sem.at[k, which], vr_sem.at[k, which], at(core_to=1 - core))
    for fetch in fetches[6:]:
        fetch.wait()
    for copy in earlier:
        copy.wait_send()
    for copy in a_copies.values():
        copy.wait_recv()
    by_step = [
        jnp.concatenate([abuf[j, 2 * head + step] for j in range(NX) for head in range(2)], axis=1) for step in range(2)
    ]
    features = jnp.concatenate(by_step, axis=0)

    def partial(which):
        for k in range(1, NX):
            v_copies[k, which].wait_recv()
        found = nn_dot(features, w_ref[which].reshape(NX * w_rows, columns))
        return found.reshape(2, rows, columns)

    there = partial(0)
    hsend[...] = there.astype(jnp.bfloat16)
    h_copies = []
    for step in range(2):
        h_copies.append(send(hsend.at[step], hrecv.at[step], hs_sem.at[step], hr_sem.at[step], at(zh_to=1 - zh)))
    here = partial(1)
    for copy in [*a_copies.values(), *v_copies.values()]:
        copy.wait_send()
    for step in range(2):
        h_copies[step].wait_recv()
        out_ref[step] = here[step] + hrecv[step].astype(jnp.float32)
    for copy in h_copies:
        copy.wait_send()


def per_device(queries, new_keys, new_values, prev_keys, prev_values, kv_basis, out_weight, out_gate):
    steps, rows, _ = queries.shape
    columns = out_gate.shape[1]
    bf16, f32 = jnp.bfloat16, jnp.float32
    vmem = pl.BlockSpec(memory_space=pltpu.VMEM)
    dma = pltpu.SemaphoreType.DMA
    tokens = 2 * NY * NZ * rows
    operands = (
        queries, new_keys, new_values, prev_keys, prev_values, jnp.swapaxes(kv_basis, 2, 3), out_weight,
    )
    summed = pl.pallas_call(
        kernel,
        out_shape=jax.ShapeDtypeStruct((steps, rows, columns), f32),
        in_specs=[pl.BlockSpec(memory_space=pltpu.HBM)] * 7,
        out_specs=vmem,
        scratch_shapes=[
            *[pltpu.VMEM(operand.shape, bf16) for operand in operands[:6]],
            pltpu.VMEM((2, NX, out_weight.shape[0], columns), bf16),
            pltpu.VMEM((NZ, 3, rows, HD), bf16),
            pltpu.VMEM((2, NY, NZ, 2, rows, HD), bf16),
            pltpu.VMEM((NZ, rows, HD), bf16),
            pltpu.VMEM((NZ * rows, tokens), f32),
            pltpu.VMEM((NZ * rows, tokens), bf16),
            pltpu.VMEM((NZ, rows, HD), bf16),
            pltpu.VMEM((NX, NZ, rows, HD), bf16),
            pltpu.VMEM((steps, rows, columns), bf16),
            pltpu.VMEM((steps, rows, columns), bf16),
            dma((8,)),
            dma((NZ,)), dma((NZ,)), dma((NZ,)), dma((NZ,)),
            dma((2, HALF, CHUNKS)), dma((2, HALF, CHUNKS)),
            dma((NY, 2)), dma((NY, 2)),
            dma((CHUNKS,)), dma((CHUNKS,)),
            dma((NZ, NX)), dma((NZ, NX)),
            dma((NX, 2)), dma((NX, 2)), dma((NX, 2)), dma((NX, 2)),
            dma((2,)), dma((2,)),
        ],
        compiler_params=pltpu.CompilerParams(
            collective_id=0, has_side_effects=True, vmem_limit_bytes=32 * 1024 * 1024
        ),
    )(*[pltpu.with_memory_space_constraint(operand, pltpu.HBM) for operand in operands])
    return (out_gate[:, None, :] * summed).astype(bf16)


def solution(mesh):
    placed = (
        P(None, "patch", "tp"),
        P(None, "patch", "tp"),
        P(None, "patch", "tp"),
        P("patch", "tp"),
        P("patch", "tp"),
        P(None, "tp", None, None),
        P("tp", None),
        P(None, "tp"),
    )
    return jax.shard_map(
        per_device, mesh=mesh, in_specs=placed, out_specs=P(None, "patch", "tp"), check_vma=False
    )
```

```python
import functools

import jax
import jax.numpy as jnp
from jax import lax
from jax.experimental import pallas as pl
from jax.experimental.pallas import tpu as pltpu
from jax.sharding import PartitionSpec as P

MESH = pl.DeviceIdType.MESH
NZ = 4
NY = 8
NX = 4
HD = 128
CHUNKS = 2
PER = NZ // CHUNKS
HALF = NY // 2


def slot_of(way, distance):
    if distance == 0 or distance == HALF:
        return 2 * distance - (distance == HALF)
    return 2 * distance - 1 + way


def far_way(chunk):
    return 0 if chunk < CHUNKS // 2 else 1


def nt_dot(a, b):
    return lax.dot_general(a, b, (((1,), (1,)), ((), ())), preferred_element_type=jnp.float32)


def nn_dot(a, b):
    return jnp.dot(a, b, preferred_element_type=jnp.float32)


def kernel(
    q_hbm, nk_hbm, nv_hbm, pk_hbm, pv_hbm, basis_hbm, w_hbm, out_ref,
    q_ref, nk_ref, nv_ref, pk_ref, pv_ref, basis_ref, w_ref,
    zsend, kv, qbuf, scores, weights, asend, abuf, hsend, hrecv,
    in_sem, zs_sem, zr_sem, qs_sem, qr_sem, rs_sem, rr_sem, cs_sem, cr_sem,
    fs_sem, fr_sem, as_sem, ar_sem, ws_sem, wr_sem, vs_sem, vr_sem, hs_sem, hr_sem,
):
    rows = pk_ref.shape[0]
    columns = out_ref.shape[2]
    patch, tp = lax.axis_index("patch"), lax.axis_index("tp")
    core = patch % 2
    y = (patch // 2) % NY
    z = patch // (2 * NY)
    x = tp % NX
    zh = tp // NX

    def at(z_to=None, y_to=None, core_to=None, x_to=None, zh_to=None):
        z_t = z if z_to is None else z_to
        y_t = y if y_to is None else y_to
        c_t = core if core_to is None else core_to
        x_t = x if x_to is None else x_to
        h_t = zh if zh_to is None else zh_to
        return ((z_t * NY + y_t) * 2 + c_t, h_t * NX + x_t)

    z_peers = [lax.rem(z + k, NZ) for k in range(NZ)]
    z_back = [lax.rem(z + NZ - k, NZ) for k in range(NZ)]
    x_peers = [lax.rem(x + k, NX) for k in range(NX)]
    x_back = [lax.rem(x + NX - k, NX) for k in range(NX)]
    y_next = [lax.rem(y + 1, NY), lax.rem(y + NY - 1, NY)]
    y_after = [lax.rem(y + 2, NY), lax.rem(y + NY - 2, NY)]

    halves = (1 - zh, zh)
    w_rows = w_hbm.shape[0]
    core_rows = pl.ds(pl.multiple_of(core * (w_rows // 2), w_rows // 2), w_rows // 2)

    def columns_of(which, x_to):
        return pl.ds(pl.multiple_of((halves[which] * NX + x_to) * columns, columns), columns)

    fetches = [
        pltpu.make_async_copy(source, target, in_sem.at[number])
        for number, (source, target) in enumerate(
            (
                (basis_hbm, basis_ref), (nk_hbm, nk_ref), (pk_hbm, pk_ref), (nv_hbm, nv_ref),
                (pv_hbm, pv_ref), (q_hbm, q_ref),
                (w_hbm.at[:, columns_of(0, x)], w_ref.at[0, x]), (w_hbm.at[:, columns_of(1, x)], w_ref.at[1, x]),
            )
        )
    ]
    for fetch in fetches:
        fetch.start()

    barrier = pltpu.get_barrier_semaphore()
    others = [(k, j) for k in range(NZ) for j in range(NX) if k or j]
    friends = [at(z_to=z_peers[k], x_to=x_peers[j]) for k, j in others]
    friends += [at(y_to=y_to[way], core_to=c) for y_to in (y_next, y_after) for way in range(2) for c in (core, 1 - core)]
    friends += [at(core_to=1 - core), at(zh_to=1 - zh)]
    for friend in friends:
        pl.semaphore_signal(barrier, inc=1, device_id=friend, device_id_type=MESH)

    for fetch in fetches[:6]:
        fetch.wait()
    chains = [(member, head) for member in range(2) for head in range(2)]
    fresh_refs, prev_refs = (nk_ref, nv_ref), (pk_ref, pv_ref)
    columns_of_head = [slice(head * HD, (head + 1) * HD) for head in range(2)]
    basis = {(member, head): basis_ref[member, head] for member, head in chains}
    shared, mapped, shared_mapped = {}, {}, {}
    for member, head in chains:
        cols = columns_of_head[head]
        shared[member, head] = prev_refs[member][:, cols]
        fresh = fresh_refs[member]
        stacked = jnp.concatenate([fresh[0, :, cols], fresh[1, :, cols], shared[member, head]], axis=0)
        mapped[member, head] = nt_dot(stacked, basis[member, head])
        shared_mapped[member, head] = mapped[member, head][2 * rows :]
    for step in range(2):
        low_rank = {}
        for chain in chains:
            coefficients = mapped[chain][step * rows : (step + 1) * rows] - shared_mapped[chain]
            low_rank[chain] = nn_dot(coefficients.astype(jnp.bfloat16), basis[chain])
        for chain in chains:
            shared[chain] = (shared[chain].astype(jnp.float32) + low_rank[chain]).astype(jnp.bfloat16)
            if step == 0:
                shared_mapped[chain] = nt_dot(shared[chain], basis[chain])
        for member, head in chains:
            zsend[2 * head + step, member] = shared[member, head]
    for head in range(2):
        for step in range(2):
            zsend[2 * head + step, 2] = q_ref[step, :, head * HD : (head + 1) * HD]


    pl.semaphore_wait(barrier, len(friends))

    started = []

    def send(src, dst, send_sem, recv_sem, device):
        copy = pltpu.make_async_remote_copy(
            src_ref=src, dst_ref=dst, send_sem=send_sem, recv_sem=recv_sem, device_id=device, device_id_type=MESH
        )
        copy.start()
        started.append(copy)
        return copy

    z_copies, q_copies = {}, {}
    for k in range(1, NZ):
        z_copies[k] = send(
            zsend.at[z_peers[k], pl.ds(0, 2)], kv.at[0, 0, k], zs_sem.at[k], zr_sem.at[k], at(z_to=z_peers[k])
        )
    w_copies = {}
    for k in (2, 1, 3):
        for which in range(2):
            w_copies[k, which] = send(
                w_hbm.at[core_rows, columns_of(which, x_peers[k])], w_ref.at[which, x, core_rows],
                ws_sem.at[k, which], wr_sem.at[k, which], at(x_to=x_peers[k]),
            )
    kv[0, 0, 0] = zsend[z, 0:2]
    qbuf[0] = zsend[z, 2]

    ring, share, cross = {}, {}, {}

    def push(way, distance, chunk, step):
        piece = pl.ds(chunk * PER, PER)
        ring[way, distance + step, chunk] = send(
            kv.at[0, slot_of(way, distance), piece],
            kv.at[0, slot_of(way, distance + step), piece],
            rs_sem.at[way, distance + step - 1, chunk],
            rr_sem.at[way, distance + step - 1, chunk],
            at(y_to=(y_next if step == 1 else y_after)[way]),
        )

    def push_both(way, chunk, step):
        push(way, HALF - 2, chunk, step)
        piece = pl.ds(chunk * PER, PER)
        distance = HALF - 2 + step
        cross[way, distance, chunk] = send(
            kv.at[0, slot_of(way, HALF - 2), piece], kv.at[1, slot_of(way, distance), piece],
            fs_sem.at[way, step - 1, chunk], fr_sem.at[way, step - 1, chunk],
            at(y_to=(y_next if step == 1 else y_after)[way], core_to=1 - core),
        )

    def share_core(slot):
        share[slot] = send(
            kv.at[0, slot], kv.at[1, slot], cs_sem.at[slot], cr_sem.at[slot], at(core_to=1 - core)
        )

    lag = 2
    for chunk in range(CHUNKS + lag):
        if chunk < CHUNKS:
            for k in range(chunk * PER, (chunk + 1) * PER):
                if k:
                    z_copies[k].wait_recv()
            for way in range(2):
                push(way, 0, chunk, 2)
        if chunk >= lag:
            for way in range(2):
                push(way, 0, chunk - lag, 1)
        if chunk == 0:
            for k in range(1, NZ):
                q_copies[k] = send(
                    zsend.at[z_peers[k], 2], qbuf.at[k], qs_sem.at[k], qr_sem.at[k], at(z_to=z_peers[k])
                )
    share_core(0)
    for k in range(1, NZ):
        q_copies[k].wait_recv()
    queries = qbuf[...].reshape(NZ * rows, HD)
    scale = HD ** (-0.5)
    block = NZ * rows
    lane_max = []

    def score(side, distance):
        first, last = slot_of(0, distance), slot_of(1, distance)
        count = last - first + 1
        keys = kv[side, first : last + 1, :, 0].reshape(count * block, HD)
        begin = (side * NY + first) * block
        found = nt_dot(queries, keys) * scale
        scores[:, begin : begin + count * block] = found
        for number in range(count):
            piece = found[:, number * block : (number + 1) * block]
            lane_max[:] = [jnp.maximum(lane_max[0], piece) if lane_max else piece]

    def score_other(distance):
        for slot in sorted({slot_of(0, distance), slot_of(1, distance)}):
            if slot in share:
                share[slot].wait_recv()
        for key, copy in cross.items():
            if key[1] == distance:
                copy.wait_recv()
        score(1, distance)

    score(0, 0)
    for chunk in range(CHUNKS):
        for way in range(2):
            ring[way, HALF - 2, chunk].wait_recv()
            push_both(way, chunk, 1)
        push_both(far_way(chunk), chunk, 2)
    for distance in (2, 1):
        for way in range(2):
            for chunk in range(CHUNKS if distance == 1 else 0):
                ring[way, distance, chunk].wait_recv()
            share_core(slot_of(way, distance))
    score(0, 2)
    score(0, 1)
    for distance in range(HALF - 1):
        score_other(distance)
    for distance in (HALF - 1, HALF):
        for key, copy in ring.items():
            if key[1] == distance:
                copy.wait_recv()
        score(0, distance)
        score_other(distance)

    earlier = list(started)
    a_copies = {}
    side_keys = NY * block
    part = block // 2
    owners = NZ // 2
    for half in (1, 0):
        own_rows = slice(half * part, (half + 1) * part)
        row_max = jnp.max(lane_max[0][own_rows], axis=1, keepdims=True)
        lane_total = jnp.zeros((part, block), jnp.float32)
        summed = jnp.zeros((part, HD), jnp.float32)
        for side in range(2):
            for index in range(side * NY, (side + 1) * NY):
                span = slice(index * block, (index + 1) * block)
                exponent = jnp.exp(scores[own_rows, span] - row_max)
                lane_total = lane_total + exponent
                weights[own_rows, span] = exponent.astype(jnp.bfloat16)
            values = kv[side, :, :, 1].reshape(side_keys, HD)
            summed += nn_dot(weights[own_rows, side * side_keys : (side + 1) * side_keys], values)
        row_total = jnp.sum(lane_total, axis=1, keepdims=True)
        attended = (summed / row_total).astype(jnp.bfloat16)
        asend[half * owners : (half + 1) * owners] = attended.reshape(owners, rows, HD)
        for j in (2, 1, 3, 0):
            for k in range(half * owners, (half + 1) * owners):
                if k or j:
                    a_copies[k, j] = send(
                        asend.at[k], abuf.at[x, z], as_sem.at[k, j], ar_sem.at[k, j], at(z_to=z_back[k], x_to=x_peers[j])
                    )
    abuf[x, z] = asend[0]

    v_copies = {}
    for which in range(2):
        for k in (1, 3, 2):
            w_copies[k, which].wait_recv()
            there = w_ref.at[which, x_back[k], core_rows]
            v_copies[k, which] = send(there, there, vs_sem.at[k, which], vr_sem.at[k, which], at(core_to=1 - core))
    for fetch in fetches[6:]:
        fetch.wait()
    for copy in earlier:
        copy.wait_send()
    for copy in a_copies.values():
        copy.wait_recv()
    by_step = [
        jnp.concatenate([abuf[j, 2 * head + step] for j in range(NX) for head in range(2)], axis=1) for step in range(2)
    ]
    features = jnp.concatenate(by_step, axis=0)

    def partial(which):
        for k in range(1, NX):
            v_copies[k, which].wait_recv()
        found = nn_dot(features, w_ref[which].reshape(NX * w_rows, columns))
        return found.reshape(2, rows, columns)

    there = partial(0)
    hsend[...] = there.astype(jnp.bfloat16)
    h_copies = []
    for step in range(2):
        h_copies.append(send(hsend.at[step], hrecv.at[step], hs_sem.at[step], hr_sem.at[step], at(zh_to=1 - zh)))
    here = partial(1)
    for copy in [*a_copies.values(), *v_copies.values()]:
        copy.wait_send()
    for step in range(2):
        h_copies[step].wait_recv()
        out_ref[step] = here[step] + hrecv[step].astype(jnp.float32)
    for copy in h_copies:
        copy.wait_send()


def per_device(queries, new_keys, new_values, prev_keys, prev_values, kv_basis, out_weight, out_gate):
    steps, rows, _ = queries.shape
    columns = out_gate.shape[1]
    bf16, f32 = jnp.bfloat16, jnp.float32
    vmem = pl.BlockSpec(memory_space=pltpu.VMEM)
    dma = pltpu.SemaphoreType.DMA
    tokens = 2 * NY * NZ * rows
    operands = (
        queries, new_keys, new_values, prev_keys, prev_values, jnp.swapaxes(kv_basis, 2, 3), out_weight,
    )
    summed = pl.pallas_call(
        kernel,
        out_shape=jax.ShapeDtypeStruct((steps, rows, columns), f32),
        in_specs=[pl.BlockSpec(memory_space=pltpu.HBM)] * 7,
        out_specs=vmem,
        scratch_shapes=[
            *[pltpu.VMEM(operand.shape, bf16) for operand in operands[:6]],
            pltpu.VMEM((2, NX, out_weight.shape[0], columns), bf16),
            pltpu.VMEM((NZ, 3, rows, HD), bf16),
            pltpu.VMEM((2, NY, NZ, 2, rows, HD), bf16),
            pltpu.VMEM((NZ, rows, HD), bf16),
            pltpu.VMEM((NZ * rows, tokens), f32),
            pltpu.VMEM((NZ * rows, tokens), bf16),
            pltpu.VMEM((NZ, rows, HD), bf16),
            pltpu.VMEM((NX, NZ, rows, HD), bf16),
            pltpu.VMEM((steps, rows, columns), bf16),
            pltpu.VMEM((steps, rows, columns), bf16),
            dma((8,)),
            dma((NZ,)), dma((NZ,)), dma((NZ,)), dma((NZ,)),
            dma((2, HALF, CHUNKS)), dma((2, HALF, CHUNKS)),
            dma((NY,)), dma((NY,)),
            dma((2, 2, CHUNKS)), dma((2, 2, CHUNKS)),
            dma((NZ, NX)), dma((NZ, NX)),
            dma((NX, 2)), dma((NX, 2)), dma((NX, 2)), dma((NX, 2)),
            dma((2,)), dma((2,)),
        ],
        compiler_params=pltpu.CompilerParams(
            collective_id=0, has_side_effects=True, vmem_limit_bytes=32 * 1024 * 1024
        ),
    )(*[pltpu.with_memory_space_constraint(operand, pltpu.HBM) for operand in operands])
    return (out_gate[:, None, :] * summed).astype(bf16)


def solution(mesh):
    placed = (
        P(None, "patch", "tp"),
        P(None, "patch", "tp"),
        P(None, "patch", "tp"),
        P("patch", "tp"),
        P("patch", "tp"),
        P(None, "tp", None, None),
        P("tp", None),
        P(None, "tp"),
    )
    return jax.shard_map(
        per_device, mesh=mesh, in_specs=placed, out_specs=P(None, "patch", "tp"), check_vma=False
    )
```

```python
import functools

import jax
import jax.numpy as jnp
from jax import lax
from jax.experimental import pallas as pl
from jax.experimental.pallas import tpu as pltpu
from jax.sharding import PartitionSpec as P

MESH = pl.DeviceIdType.MESH
NZ = 4
NY = 8
NX = 4
HD = 128
CHUNKS = 2
PER = NZ // CHUNKS
HALF = NY // 2


def slot_of(way, distance):
    if distance == 0 or distance == HALF:
        return 2 * distance - (distance == HALF)
    return 2 * distance - 1 + way


def far_way(chunk):
    return 0 if chunk < CHUNKS // 2 else 1


def nt_dot(a, b):
    return lax.dot_general(a, b, (((1,), (1,)), ((), ())), preferred_element_type=jnp.float32)


def nn_dot(a, b):
    return jnp.dot(a, b, preferred_element_type=jnp.float32)


def kernel(
    q_hbm, nk_hbm, nv_hbm, pk_hbm, pv_hbm, basis_hbm, w_hbm, out_ref,
    q_ref, nk_ref, nv_ref, pk_ref, pv_ref, basis_ref, w_ref,
    zsend, kv, qbuf, scores, weights, asend, abuf, hsend, hrecv,
    in_sem, zs_sem, zr_sem, qs_sem, qr_sem, rs_sem, rr_sem, cs_sem, cr_sem,
    fs_sem, fr_sem, as_sem, ar_sem, ws_sem, wr_sem, vs_sem, vr_sem, hs_sem, hr_sem,
):
    rows = pk_ref.shape[0]
    columns = out_ref.shape[2]
    patch, tp = lax.axis_index("patch"), lax.axis_index("tp")
    core = patch % 2
    y = (patch // 2) % NY
    z = patch // (2 * NY)
    x = tp % NX
    zh = tp // NX

    def at(z_to=None, y_to=None, core_to=None, x_to=None, zh_to=None):
        z_t = z if z_to is None else z_to
        y_t = y if y_to is None else y_to
        c_t = core if core_to is None else core_to
        x_t = x if x_to is None else x_to
        h_t = zh if zh_to is None else zh_to
        return ((z_t * NY + y_t) * 2 + c_t, h_t * NX + x_t)

    z_peers = [lax.rem(z + k, NZ) for k in range(NZ)]
    z_back = [lax.rem(z + NZ - k, NZ) for k in range(NZ)]
    x_peers = [lax.rem(x + k, NX) for k in range(NX)]
    x_back = [lax.rem(x + NX - k, NX) for k in range(NX)]
    y_next = [lax.rem(y + 1, NY), lax.rem(y + NY - 1, NY)]
    y_after = [lax.rem(y + 2, NY), lax.rem(y + NY - 2, NY)]

    halves = (1 - zh, zh)
    w_rows = w_hbm.shape[0]
    core_rows = pl.ds(pl.multiple_of(core * (w_rows // 2), w_rows // 2), w_rows // 2)

    def columns_of(which, x_to):
        return pl.ds(pl.multiple_of((halves[which] * NX + x_to) * columns, columns), columns)

    fetches = [
        pltpu.make_async_copy(source, target, in_sem.at[number])
        for number, (source, target) in enumerate(
            (
                (basis_hbm, basis_ref), (nk_hbm, nk_ref), (pk_hbm, pk_ref), (nv_hbm, nv_ref),
                (pv_hbm, pv_ref), (q_hbm, q_ref),
                (w_hbm.at[:, columns_of(0, x)], w_ref.at[0, x]), (w_hbm.at[:, columns_of(1, x)], w_ref.at[1, x]),
            )
        )
    ]
    for fetch in fetches:
        fetch.start()

    barrier = pltpu.get_barrier_semaphore()
    others = [(k, j) for k in range(NZ) for j in range(NX) if k or j]
    friends = [at(z_to=z_peers[k], x_to=x_peers[j]) for k, j in others]
    friends += [at(y_to=y_next[way]) for way in range(2)]
    friends += [at(y_to=y_after[way], core_to=c) for way in range(2) for c in (core, 1 - core)]
    friends += [at(core_to=1 - core), at(zh_to=1 - zh)]
    for friend in friends:
        pl.semaphore_signal(barrier, inc=1, device_id=friend, device_id_type=MESH)

    for fetch in fetches[:6]:
        fetch.wait()
    chains = [(member, head) for member in range(2) for head in range(2)]
    fresh_refs, prev_refs = (nk_ref, nv_ref), (pk_ref, pv_ref)
    columns_of_head = [slice(head * HD, (head + 1) * HD) for head in range(2)]
    basis = {(member, head): basis_ref[member, head] for member, head in chains}
    shared, mapped, shared_mapped = {}, {}, {}
    for member, head in chains:
        cols = columns_of_head[head]
        shared[member, head] = prev_refs[member][:, cols]
        fresh = fresh_refs[member]
        stacked = jnp.concatenate([fresh[0, :, cols], fresh[1, :, cols], shared[member, head]], axis=0)
        mapped[member, head] = nt_dot(stacked, basis[member, head])
        shared_mapped[member, head] = mapped[member, head][2 * rows :]
    for step in range(2):
        low_rank = {}
        for chain in chains:
            coefficients = mapped[chain][step * rows : (step + 1) * rows] - shared_mapped[chain]
            low_rank[chain] = nn_dot(coefficients.astype(jnp.bfloat16), basis[chain])
        for chain in chains:
            shared[chain] = (shared[chain].astype(jnp.float32) + low_rank[chain]).astype(jnp.bfloat16)
            if step == 0:
                shared_mapped[chain] = nt_dot(shared[chain], basis[chain])
        for member, head in chains:
            zsend[2 * head + step, member] = shared[member, head]
    for head in range(2):
        for step in range(2):
            zsend[2 * head + step, 2] = q_ref[step, :, head * HD : (head + 1) * HD]


    pl.semaphore_wait(barrier, len(friends))

    started = []

    def send(src, dst, send_sem, recv_sem, device):
        copy = pltpu.make_async_remote_copy(
            src_ref=src, dst_ref=dst, send_sem=send_sem, recv_sem=recv_sem, device_id=device, device_id_type=MESH
        )
        copy.start()
        started.append(copy)
        return copy

    z_copies, q_copies = {}, {}
    for k in range(1, NZ):
        z_copies[k] = send(
            zsend.at[z_peers[k], pl.ds(0, 2)], kv.at[0, 0, k], zs_sem.at[k], zr_sem.at[k], at(z_to=z_peers[k])
        )
    w_copies = {}
    for k in (2, 1, 3):
        for which in range(2):
            w_copies[k, which] = send(
                w_hbm.at[core_rows, columns_of(which, x_peers[k])], w_ref.at[which, x, core_rows],
                ws_sem.at[k, which], wr_sem.at[k, which], at(x_to=x_peers[k]),
            )
    kv[0, 0, 0] = zsend[z, 0:2]
    qbuf[0] = zsend[z, 2]

    ring, share, far_other = {}, {}, {}

    def push(way, distance, chunk, step):
        piece = pl.ds(chunk * PER, PER)
        ring[way, distance + step, chunk] = send(
            kv.at[0, slot_of(way, distance), piece],
            kv.at[0, slot_of(way, distance + step), piece],
            rs_sem.at[way, distance + step - 1, chunk],
            rr_sem.at[way, distance + step - 1, chunk],
            at(y_to=(y_next if step == 1 else y_after)[way]),
        )

    def far_push(way, chunk):
        push(way, HALF - 2, chunk, 2)
        piece = pl.ds(chunk * PER, PER)
        far_other[chunk] = send(
            kv.at[0, slot_of(way, HALF - 2), piece], kv.at[1, slot_of(0, HALF), piece],
            fs_sem.at[chunk], fr_sem.at[chunk], at(y_to=y_after[way], core_to=1 - core),
        )

    def share_core(way, distance, chunk):
        parts = 1 if distance < HALF - 1 else 2
        count = CHUNKS // parts
        if (chunk + 1) % count:
            return
        part = chunk // count
        piece = pl.ds(part * count * PER, count * PER)
        slot = slot_of(way, distance)
        share[slot, part] = send(
            kv.at[0, slot, piece],
            kv.at[1, slot, piece],
            cs_sem.at[slot, part],
            cr_sem.at[slot, part],
            at(core_to=1 - core),
        )

    lag = 2
    for chunk in range(CHUNKS + lag):
        if chunk < CHUNKS:
            for k in range(chunk * PER, (chunk + 1) * PER):
                if k:
                    z_copies[k].wait_recv()
            for way in range(2):
                push(way, 0, chunk, 2)
            share_core(0, 0, chunk)
        if chunk >= lag:
            for way in range(2):
                push(way, 0, chunk - lag, 1)
        if chunk == 0:
            for k in range(1, NZ):
                q_copies[k] = send(
                    zsend.at[z_peers[k], 2], qbuf.at[k], qs_sem.at[k], qr_sem.at[k], at(z_to=z_peers[k])
                )
    for k in range(1, NZ):
        q_copies[k].wait_recv()
    queries = qbuf[...].reshape(NZ * rows, HD)
    scale = HD ** (-0.5)
    block = NZ * rows
    lane_max = {}

    def group_of(distance):
        return int(distance >= HALF - 1)

    def score(side, distance):
        first, last = slot_of(0, distance), slot_of(1, distance)
        count = last - first + 1
        keys = kv[side, first : last + 1, :, 0].reshape(count * block, HD)
        begin = (side * NY + first) * block
        found = nt_dot(queries, keys) * scale
        scores[:, begin : begin + count * block] = found
        for number in range(count):
            piece = found[:, number * block : (number + 1) * block]
            group = group_of(distance)
            lane_max[group] = jnp.maximum(lane_max[group], piece) if group in lane_max else piece

    def score_other(distance):
        for slot in sorted({slot_of(0, distance), slot_of(1, distance)}):
            for part in range(2):
                if (slot, part) in share:
                    share[slot, part].wait_recv()
        for chunk in range(CHUNKS if distance == HALF else 0):
            far_other[chunk].wait_recv()
        score(1, distance)

    score(0, 0)
    for chunk in range(CHUNKS):
        for way in range(2):
            ring[way, HALF - 2, chunk].wait_recv()
            push(way, HALF - 2, chunk, 1)
        far_push(far_way(chunk), chunk)
        for way in range(2):
            share_core(way, HALF - 2, chunk)
    for chunk in range(CHUNKS):
        for way in range(2):
            ring[way, 1, chunk].wait_recv()
            share_core(way, 1, chunk)
    score(0, 2)
    score(0, 1)
    score_other(0)
    def weigh(group, row_max):
        slots = [slot_of(way, distance) for distance in range(HALF + 1) for way in range(2) if group_of(distance) == group]
        first, last = min(slots), max(slots)
        count = last - first + 1
        lane_total = jnp.zeros((block, block), jnp.float32)
        summed = jnp.zeros((block, HD), jnp.float32)
        for side in range(2):
            begin = (side * NY + first) * block
            for number in range(count):
                span = slice(begin + number * block, begin + (number + 1) * block)
                exponent = jnp.exp(scores[:, span] - row_max)
                lane_total = lane_total + exponent
                weights[:, span] = exponent.astype(jnp.bfloat16)
            values = kv[side, first : last + 1, :, 1].reshape(count * block, HD)
            summed = summed + nn_dot(weights[:, begin : begin + count * block], values)
        return lane_total, summed

    def share_last():
        for chunk in range(CHUNKS):
            for way in range(2):
                ring[way, HALF - 1, chunk].wait_recv()
                share_core(way, HALF - 1, chunk)

    score_other(2)
    score_other(1)
    near_max = jnp.max(lane_max[0], axis=1, keepdims=True)
    near_total, near_summed = weigh(0, near_max)
    share_last()
    score(0, HALF - 1)
    for chunk in range(CHUNKS):
        ring[far_way(chunk), HALF, chunk].wait_recv()
    score(0, HALF)
    score_other(HALF)
    score_other(HALF - 1)

    row_max = jnp.maximum(near_max, jnp.max(lane_max[1], axis=1, keepdims=True))
    rescale = jnp.exp(near_max - row_max)
    far_total, far_summed = weigh(1, row_max)
    row_total = jnp.sum(near_total * rescale + far_total, axis=1, keepdims=True)
    attended = ((near_summed * rescale + far_summed) / row_total).astype(jnp.bfloat16)
    asend[...] = attended.reshape(NZ, rows, HD)

    earlier = list(started)
    a_copies = {}
    for j in (2, 1, 3, 0):
        for k in (2, 1, 3, 0):
            if k or j:
                a_copies[k, j] = send(
                    asend.at[k], abuf.at[x, z], as_sem.at[k, j], ar_sem.at[k, j], at(z_to=z_back[k], x_to=x_peers[j])
                )
    abuf[x, z] = asend[0]

    v_copies = {}
    for which in range(2):
        for k in (1, 3, 2):
            w_copies[k, which].wait_recv()
            there = w_ref.at[which, x_back[k], core_rows]
            v_copies[k, which] = send(there, there, vs_sem.at[k, which], vr_sem.at[k, which], at(core_to=1 - core))
    for fetch in fetches[6:]:
        fetch.wait()
    for copy in earlier:
        copy.wait_send()
    for copy in a_copies.values():
        copy.wait_recv()
    by_step = [
        jnp.concatenate([abuf[j, 2 * head + step] for j in range(NX) for head in range(2)], axis=1) for step in range(2)
    ]
    features = jnp.concatenate(by_step, axis=0)

    def partial(which):
        for k in range(1, NX):
            v_copies[k, which].wait_recv()
        found = nn_dot(features, w_ref[which].reshape(NX * w_rows, columns))
        return found.reshape(2, rows, columns)

    there = partial(0)
    hsend[...] = there.astype(jnp.bfloat16)
    h_copies = []
    for step in range(2):
        h_copies.append(send(hsend.at[step], hrecv.at[step], hs_sem.at[step], hr_sem.at[step], at(zh_to=1 - zh)))
    here = partial(1)
    for copy in [*a_copies.values(), *v_copies.values()]:
        copy.wait_send()
    for step in range(2):
        h_copies[step].wait_recv()
        out_ref[step] = here[step] + hrecv[step].astype(jnp.float32)
    for copy in h_copies:
        copy.wait_send()


def per_device(queries, new_keys, new_values, prev_keys, prev_values, kv_basis, out_weight, out_gate):
    steps, rows, _ = queries.shape
    columns = out_gate.shape[1]
    bf16, f32 = jnp.bfloat16, jnp.float32
    vmem = pl.BlockSpec(memory_space=pltpu.VMEM)
    dma = pltpu.SemaphoreType.DMA
    tokens = 2 * NY * NZ * rows
    operands = (
        queries, new_keys, new_values, prev_keys, prev_values, jnp.swapaxes(kv_basis, 2, 3), out_weight,
    )
    summed = pl.pallas_call(
        kernel,
        out_shape=jax.ShapeDtypeStruct((steps, rows, columns), f32),
        in_specs=[pl.BlockSpec(memory_space=pltpu.HBM)] * 7,
        out_specs=vmem,
        scratch_shapes=[
            *[pltpu.VMEM(operand.shape, bf16) for operand in operands[:6]],
            pltpu.VMEM((2, NX, out_weight.shape[0], columns), bf16),
            pltpu.VMEM((NZ, 3, rows, HD), bf16),
            pltpu.VMEM((2, NY, NZ, 2, rows, HD), bf16),
            pltpu.VMEM((NZ, rows, HD), bf16),
            pltpu.VMEM((NZ * rows, tokens), f32),
            pltpu.VMEM((NZ * rows, tokens), bf16),
            pltpu.VMEM((NZ, rows, HD), bf16),
            pltpu.VMEM((NX, NZ, rows, HD), bf16),
            pltpu.VMEM((steps, rows, columns), bf16),
            pltpu.VMEM((steps, rows, columns), bf16),
            dma((8,)),
            dma((NZ,)), dma((NZ,)), dma((NZ,)), dma((NZ,)),
            dma((2, HALF, CHUNKS)), dma((2, HALF, CHUNKS)),
            dma((NY, 2)), dma((NY, 2)),
            dma((CHUNKS,)), dma((CHUNKS,)),
            dma((NZ, NX)), dma((NZ, NX)),
            dma((NX, 2)), dma((NX, 2)), dma((NX, 2)), dma((NX, 2)),
            dma((2,)), dma((2,)),
        ],
        compiler_params=pltpu.CompilerParams(
            collective_id=0, has_side_effects=True, vmem_limit_bytes=32 * 1024 * 1024
        ),
    )(*[pltpu.with_memory_space_constraint(operand, pltpu.HBM) for operand in operands])
    return (out_gate[:, None, :] * summed).astype(bf16)


def solution(mesh):
    placed = (
        P(None, "patch", "tp"),
        P(None, "patch", "tp"),
        P(None, "patch", "tp"),
        P("patch", "tp"),
        P("patch", "tp"),
        P(None, "tp", None, None),
        P("tp", None),
        P(None, "tp"),
    )
    return jax.shard_map(
        per_device, mesh=mesh, in_specs=placed, out_specs=P(None, "patch", "tp"), check_vma=False
    )
```

```python
import functools

import jax
import jax.numpy as jnp
from jax import lax
from jax.experimental import pallas as pl
from jax.experimental.pallas import tpu as pltpu
from jax.sharding import PartitionSpec as P

MESH = pl.DeviceIdType.MESH
NZ = 4
NY = 8
NX = 4
HD = 128
CHUNKS = 2
PER = NZ // CHUNKS
HALF = NY // 2


def slot_of(way, distance):
    if distance == 0 or distance == HALF:
        return 2 * distance - (distance == HALF)
    return 2 * distance - 1 + way


def far_way(chunk):
    return 0 if chunk < CHUNKS // 2 else 1


def nt_dot(a, b):
    return lax.dot_general(a, b, (((1,), (1,)), ((), ())), preferred_element_type=jnp.float32)


def nn_dot(a, b):
    return jnp.dot(a, b, preferred_element_type=jnp.float32)


def kernel(
    q_hbm, nk_hbm, nv_hbm, pk_hbm, pv_hbm, basis_hbm, w_hbm, out_ref,
    q_ref, nk_ref, nv_ref, pk_ref, pv_ref, basis_ref, w_ref,
    zsend, kv, qbuf, scores, weights, asend, abuf, hsend, hrecv,
    in_sem, zs_sem, zr_sem, qs_sem, qr_sem, rs_sem, rr_sem, cs_sem, cr_sem,
    fs_sem, fr_sem, as_sem, ar_sem, ws_sem, wr_sem, vs_sem, vr_sem, hs_sem, hr_sem,
):
    rows = pk_ref.shape[0]
    columns = out_ref.shape[2]
    patch, tp = lax.axis_index("patch"), lax.axis_index("tp")
    core = patch % 2
    y = (patch // 2) % NY
    z = patch // (2 * NY)
    x = tp % NX
    zh = tp // NX

    def at(z_to=None, y_to=None, core_to=None, x_to=None, zh_to=None):
        z_t = z if z_to is None else z_to
        y_t = y if y_to is None else y_to
        c_t = core if core_to is None else core_to
        x_t = x if x_to is None else x_to
        h_t = zh if zh_to is None else zh_to
        return ((z_t * NY + y_t) * 2 + c_t, h_t * NX + x_t)

    z_peers = [lax.rem(z + k, NZ) for k in range(NZ)]
    z_back = [lax.rem(z + NZ - k, NZ) for k in range(NZ)]
    x_peers = [lax.rem(x + k, NX) for k in range(NX)]
    x_back = [lax.rem(x + NX - k, NX) for k in range(NX)]
    y_next = [lax.rem(y + 1, NY), lax.rem(y + NY - 1, NY)]
    y_after = [lax.rem(y + 2, NY), lax.rem(y + NY - 2, NY)]

    halves = (1 - zh, zh)
    w_rows = w_hbm.shape[0]
    core_rows = pl.ds(pl.multiple_of(core * (w_rows // 2), w_rows // 2), w_rows // 2)

    def columns_of(which, x_to):
        return pl.ds(pl.multiple_of((halves[which] * NX + x_to) * columns, columns), columns)

    fetches = [
        pltpu.make_async_copy(source, target, in_sem.at[number])
        for number, (source, target) in enumerate(
            (
                (basis_hbm, basis_ref), (nk_hbm, nk_ref), (pk_hbm, pk_ref), (nv_hbm, nv_ref),
                (pv_hbm, pv_ref), (q_hbm, q_ref),
                (w_hbm.at[:, columns_of(0, x)], w_ref.at[0, x]), (w_hbm.at[:, columns_of(1, x)], w_ref.at[1, x]),
            )
        )
    ]
    for fetch in fetches:
        fetch.start()

    barrier = pltpu.get_barrier_semaphore()
    others = [(k, j) for k in range(NZ) for j in range(NX) if k or j]
    friends = [at(z_to=z_peers[k], x_to=x_peers[j]) for k, j in others]
    friends += [at(y_to=y_next[way]) for way in range(2)]
    friends += [at(y_to=y_after[way], core_to=c) for way in range(2) for c in (core, 1 - core)]
    friends += [at(core_to=1 - core), at(zh_to=1 - zh)]
    for friend in friends:
        pl.semaphore_signal(barrier, inc=1, device_id=friend, device_id_type=MESH)

    for fetch in fetches[:6]:
        fetch.wait()
    chains = [(member, head) for member in range(2) for head in range(2)]
    fresh_refs, prev_refs = (nk_ref, nv_ref), (pk_ref, pv_ref)
    columns_of_head = [slice(head * HD, (head + 1) * HD) for head in range(2)]
    basis = {(member, head): basis_ref[member, head] for member, head in chains}
    shared, mapped, shared_mapped = {}, {}, {}
    for member, head in chains:
        cols = columns_of_head[head]
        shared[member, head] = prev_refs[member][:, cols]
        fresh = fresh_refs[member]
        stacked = jnp.concatenate([fresh[0, :, cols], fresh[1, :, cols], shared[member, head]], axis=0)
        mapped[member, head] = nt_dot(stacked, basis[member, head])
        shared_mapped[member, head] = mapped[member, head][2 * rows :]
    for step in range(2):
        low_rank = {}
        for chain in chains:
            coefficients = mapped[chain][step * rows : (step + 1) * rows] - shared_mapped[chain]
            low_rank[chain] = nn_dot(coefficients.astype(jnp.bfloat16), basis[chain])
        for chain in chains:
            shared[chain] = (shared[chain].astype(jnp.float32) + low_rank[chain]).astype(jnp.bfloat16)
            if step == 0:
                shared_mapped[chain] = nt_dot(shared[chain], basis[chain])
        for member, head in chains:
            zsend[2 * head + step, member] = shared[member, head]
    for head in range(2):
        for step in range(2):
            zsend[2 * head + step, 2] = q_ref[step, :, head * HD : (head + 1) * HD]


    pl.semaphore_wait(barrier, len(friends))

    started = []

    def send(src, dst, send_sem, recv_sem, device):
        copy = pltpu.make_async_remote_copy(
            src_ref=src, dst_ref=dst, send_sem=send_sem, recv_sem=recv_sem, device_id=device, device_id_type=MESH
        )
        copy.start()
        started.append(copy)
        return copy

    z_copies, q_copies = {}, {}
    for k in range(1, NZ):
        z_copies[k] = send(
            zsend.at[z_peers[k], pl.ds(0, 2)], kv.at[0, 0, k], zs_sem.at[k], zr_sem.at[k], at(z_to=z_peers[k])
        )
    w_copies = {}
    for which in range(2):
        for k in (2, 1, 3):
            w_copies[k, which] = send(
                w_hbm.at[core_rows, columns_of(which, x_peers[k])], w_ref.at[which, x, core_rows],
                ws_sem.at[k, which], wr_sem.at[k, which], at(x_to=x_peers[k]),
            )
    kv[0, 0, 0] = zsend[z, 0:2]
    qbuf[0] = zsend[z, 2]

    ring, share, far_other = {}, {}, {}

    def push(way, distance, chunk, step):
        piece = pl.ds(chunk * PER, PER)
        ring[way, distance + step, chunk] = send(
            kv.at[0, slot_of(way, distance), piece],
            kv.at[0, slot_of(way, distance + step), piece],
            rs_sem.at[way, distance + step - 1, chunk],
            rr_sem.at[way, distance + step - 1, chunk],
            at(y_to=(y_next if step == 1 else y_after)[way]),
        )

    def far_push(way, chunk):
        push(way, HALF - 2, chunk, 2)
        piece = pl.ds(chunk * PER, PER)
        far_other[chunk] = send(
            kv.at[0, slot_of(way, HALF - 2), piece], kv.at[1, slot_of(0, HALF), piece],
            fs_sem.at[chunk], fr_sem.at[chunk], at(y_to=y_after[way], core_to=1 - core),
        )

    def share_core(way, distance, chunk):
        parts = 1 if distance < HALF - 1 else 2
        count = CHUNKS // parts
        if (chunk + 1) % count:
            return
        part = chunk // count
        piece = pl.ds(part * count * PER, count * PER)
        slot = slot_of(way, distance)
        share[slot, part] = send(
            kv.at[0, slot, piece],
            kv.at[1, slot, piece],
            cs_sem.at[slot, part],
            cr_sem.at[slot, part],
            at(core_to=1 - core),
        )

    lag = 2
    for chunk in range(CHUNKS + lag):
        if chunk < CHUNKS:
            for k in range(chunk * PER, (chunk + 1) * PER):
                if k:
                    z_copies[k].wait_recv()
            for way in range(2):
                push(way, 0, chunk, 2)
            share_core(0, 0, chunk)
        if chunk >= lag:
            for way in range(2):
                push(way, 0, chunk - lag, 1)
        if chunk == 0:
            for k in range(1, NZ):
                q_copies[k] = send(
                    zsend.at[z_peers[k], 2], qbuf.at[k], qs_sem.at[k], qr_sem.at[k], at(z_to=z_peers[k])
                )
    for k in range(1, NZ):
        q_copies[k].wait_recv()
    queries = qbuf[...].reshape(NZ * rows, HD)
    scale = HD ** (-0.5)
    block = NZ * rows
    lane_max = {}

    def group_of(distance):
        return int(distance >= HALF - 1)

    def score(side, distance):
        first, last = slot_of(0, distance), slot_of(1, distance)
        count = last - first + 1
        keys = kv[side, first : last + 1, :, 0].reshape(count * block, HD)
        begin = (side * NY + first) * block
        found = nt_dot(queries, keys) * scale
        scores[:, begin : begin + count * block] = found
        for number in range(count):
            piece = found[:, number * block : (number + 1) * block]
            group = group_of(distance)
            lane_max[group] = jnp.maximum(lane_max[group], piece) if group in lane_max else piece

    def score_other(distance):
        for slot in sorted({slot_of(0, distance), slot_of(1, distance)}):
            for part in range(2):
                if (slot, part) in share:
                    share[slot, part].wait_recv()
        for chunk in range(CHUNKS if distance == HALF else 0):
            far_other[chunk].wait_recv()
        score(1, distance)

    score(0, 0)
    for chunk in range(CHUNKS):
        for way in range(2):
            ring[way, HALF - 2, chunk].wait_recv()
            push(way, HALF - 2, chunk, 1)
        far_push(far_way(chunk), chunk)
        for way in range(2):
            share_core(way, HALF - 2, chunk)
    for chunk in range(CHUNKS):
        for way in range(2):
            ring[way, 1, chunk].wait_recv()
            share_core(way, 1, chunk)
    score(0, 2)
    score(0, 1)
    score_other(0)
    def weigh(group, row_max):
        slots = [slot_of(way, distance) for distance in range(HALF + 1) for way in range(2) if group_of(distance) == group]
        first, last = min(slots), max(slots)
        count = last - first + 1
        lane_total = jnp.zeros((block, block), jnp.float32)
        summed = jnp.zeros((block, HD), jnp.float32)
        for side in range(2):
            begin = (side * NY + first) * block
            for number in range(count):
                span = slice(begin + number * block, begin + (number + 1) * block)
                exponent = jnp.exp(scores[:, span] - row_max)
                lane_total = lane_total + exponent
                weights[:, span] = exponent.astype(jnp.bfloat16)
            values = kv[side, first : last + 1, :, 1].reshape(count * block, HD)
            summed = summed + nn_dot(weights[:, begin : begin + count * block], values)
        return lane_total, summed

    def share_last():
        for chunk in range(CHUNKS):
            for way in range(2):
                ring[way, HALF - 1, chunk].wait_recv()
                share_core(way, HALF - 1, chunk)

    score_other(2)
    score_other(1)
    near_max = jnp.max(lane_max[0], axis=1, keepdims=True)
    near_total, near_summed = weigh(0, near_max)
    share_last()
    score(0, HALF - 1)
    for chunk in range(CHUNKS):
        ring[far_way(chunk), HALF, chunk].wait_recv()
    score(0, HALF)
    score_other(HALF)
    score_other(HALF - 1)

    row_max = jnp.maximum(near_max, jnp.max(lane_max[1], axis=1, keepdims=True))
    rescale = jnp.exp(near_max - row_max)
    far_total, far_summed = weigh(1, row_max)
    row_total = jnp.sum(near_total * rescale + far_total, axis=1, keepdims=True)
    attended = ((near_summed * rescale + far_summed) / row_total).astype(jnp.bfloat16)
    asend[...] = attended.reshape(NZ, rows, HD)

    a_copies = {}
    for j in (2, 1, 3, 0):
        for k in (2, 1, 3, 0):
            if k or j:
                a_copies[k, j] = send(
                    asend.at[k], abuf.at[x, z], as_sem.at[k, j], ar_sem.at[k, j], at(z_to=z_back[k], x_to=x_peers[j])
                )
    abuf[x, z] = asend[0]

    v_copies = {}

    def share_weights(which):
        for k in (1, 3, 2):
            w_copies[k, which].wait_recv()
            there = w_ref.at[which, x_back[k], core_rows]
            v_copies[k, which] = send(there, there, vs_sem.at[k, which], vr_sem.at[k, which], at(core_to=1 - core))

    def partial(which):
        fetches[6 + which].wait()
        for k in range(1, NX):
            v_copies[k, which].wait_recv()
        found = nn_dot(features, w_ref[which].reshape(NX * w_rows, columns))
        return found.reshape(2, rows, columns)

    share_weights(0)
    for copy in a_copies.values():
        copy.wait_recv()
    by_step = [
        jnp.concatenate([abuf[j, 2 * head + step] for j in range(NX) for head in range(2)], axis=1) for step in range(2)
    ]
    features = jnp.concatenate(by_step, axis=0)
    hsend[...] = partial(0).astype(jnp.bfloat16)
    h_copies = []
    for step in range(2):
        h_copies.append(send(hsend.at[step], hrecv.at[step], hs_sem.at[step], hr_sem.at[step], at(zh_to=1 - zh)))
    share_weights(1)
    here = partial(1)
    for copy in started:
        copy.wait_send()
    for step in range(2):
        h_copies[step].wait_recv()
        out_ref[step] = here[step] + hrecv[step].astype(jnp.float32)


def per_device(queries, new_keys, new_values, prev_keys, prev_values, kv_basis, out_weight, out_gate):
    steps, rows, _ = queries.shape
    columns = out_gate.shape[1]
    bf16, f32 = jnp.bfloat16, jnp.float32
    vmem = pl.BlockSpec(memory_space=pltpu.VMEM)
    dma = pltpu.SemaphoreType.DMA
    tokens = 2 * NY * NZ * rows
    operands = (
        queries, new_keys, new_values, prev_keys, prev_values, jnp.swapaxes(kv_basis, 2, 3), out_weight,
    )
    summed = pl.pallas_call(
        kernel,
        out_shape=jax.ShapeDtypeStruct((steps, rows, columns), f32),
        in_specs=[pl.BlockSpec(memory_space=pltpu.HBM)] * 7,
        out_specs=vmem,
        scratch_shapes=[
            *[pltpu.VMEM(operand.shape, bf16) for operand in operands[:6]],
            pltpu.VMEM((2, NX, out_weight.shape[0], columns), bf16),
            pltpu.VMEM((NZ, 3, rows, HD), bf16),
            pltpu.VMEM((2, NY, NZ, 2, rows, HD), bf16),
            pltpu.VMEM((NZ, rows, HD), bf16),
            pltpu.VMEM((NZ * rows, tokens), f32),
            pltpu.VMEM((NZ * rows, tokens), bf16),
            pltpu.VMEM((NZ, rows, HD), bf16),
            pltpu.VMEM((NX, NZ, rows, HD), bf16),
            pltpu.VMEM((steps, rows, columns), bf16),
            pltpu.VMEM((steps, rows, columns), bf16),
            dma((8,)),
            dma((NZ,)), dma((NZ,)), dma((NZ,)), dma((NZ,)),
            dma((2, HALF, CHUNKS)), dma((2, HALF, CHUNKS)),
            dma((NY, 2)), dma((NY, 2)),
            dma((CHUNKS,)), dma((CHUNKS,)),
            dma((NZ, NX)), dma((NZ, NX)),
            dma((NX, 2)), dma((NX, 2)), dma((NX, 2)), dma((NX, 2)),
            dma((2,)), dma((2,)),
        ],
        compiler_params=pltpu.CompilerParams(
            collective_id=0, has_side_effects=True, vmem_limit_bytes=32 * 1024 * 1024
        ),
    )(*[pltpu.with_memory_space_constraint(operand, pltpu.HBM) for operand in operands])
    return (out_gate[:, None, :] * summed).astype(bf16)


def solution(mesh):
    placed = (
        P(None, "patch", "tp"),
        P(None, "patch", "tp"),
        P(None, "patch", "tp"),
        P("patch", "tp"),
        P("patch", "tp"),
        P(None, "tp", None, None),
        P("tp", None),
        P(None, "tp"),
    )
    return jax.shard_map(
        per_device, mesh=mesh, in_specs=placed, out_specs=P(None, "patch", "tp"), check_vma=False
    )
```

```python
import functools

import jax
import jax.numpy as jnp
from jax import lax
from jax.experimental import pallas as pl
from jax.experimental.pallas import tpu as pltpu
from jax.sharding import PartitionSpec as P

MESH = pl.DeviceIdType.MESH
NZ = 4
NY = 8
NX = 4
HD = 128
CHUNKS = 2
PER = NZ // CHUNKS
HALF = NY // 2


def slot_of(way, distance):
    if distance == 0 or distance == HALF:
        return 2 * distance - (distance == HALF)
    return 2 * distance - 1 + way


def far_way(chunk):
    return 0 if chunk < CHUNKS // 2 else 1


def nt_dot(a, b):
    return lax.dot_general(a, b, (((1,), (1,)), ((), ())), preferred_element_type=jnp.float32)


def nn_dot(a, b):
    return jnp.dot(a, b, preferred_element_type=jnp.float32)


def kernel(
    q_hbm, nk_hbm, nv_hbm, pk_hbm, pv_hbm, basis_hbm, w_hbm, out_ref,
    q_ref, nk_ref, nv_ref, pk_ref, pv_ref, basis_ref, w_ref,
    diagonal, zsend, kv, qbuf, scores, weights, asend, abuf, hsend, hrecv,
    in_sem, zs_sem, zr_sem, qs_sem, qr_sem, rs_sem, rr_sem, cs_sem, cr_sem,
    fs_sem, fr_sem, as_sem, ar_sem, ws_sem, wr_sem, vs_sem, vr_sem, hs_sem, hr_sem,
):
    rows = pk_ref.shape[0]
    columns = out_ref.shape[2]
    patch, tp = lax.axis_index("patch"), lax.axis_index("tp")
    core = patch % 2
    y = (patch // 2) % NY
    z = patch // (2 * NY)
    x = tp % NX
    zh = tp // NX

    def at(z_to=None, y_to=None, core_to=None, x_to=None, zh_to=None):
        z_t = z if z_to is None else z_to
        y_t = y if y_to is None else y_to
        c_t = core if core_to is None else core_to
        x_t = x if x_to is None else x_to
        h_t = zh if zh_to is None else zh_to
        return ((z_t * NY + y_t) * 2 + c_t, h_t * NX + x_t)

    z_peers = [lax.rem(z + k, NZ) for k in range(NZ)]
    z_back = [lax.rem(z + NZ - k, NZ) for k in range(NZ)]
    x_peers = [lax.rem(x + k, NX) for k in range(NX)]
    x_back = [lax.rem(x + NX - k, NX) for k in range(NX)]
    y_next = [lax.rem(y + 1, NY), lax.rem(y + NY - 1, NY)]
    y_after = [lax.rem(y + 2, NY), lax.rem(y + NY - 2, NY)]

    halves = (1 - zh, zh)
    w_rows = w_hbm.shape[0]
    core_rows = pl.ds(pl.multiple_of(core * (w_rows // 2), w_rows // 2), w_rows // 2)

    def columns_of(which, x_to):
        return pl.ds(pl.multiple_of((halves[which] * NX + x_to) * columns, columns), columns)

    fetches = [
        pltpu.make_async_copy(source, target, in_sem.at[number])
        for number, (source, target) in enumerate(
            (
                (basis_hbm, basis_ref), (nk_hbm, nk_ref), (pk_hbm, pk_ref), (nv_hbm, nv_ref),
                (pv_hbm, pv_ref), (q_hbm, q_ref),
                (w_hbm.at[:, columns_of(0, x)], w_ref.at[0, x]), (w_hbm.at[:, columns_of(1, x)], w_ref.at[1, x]),
            )
        )
    ]
    for fetch in fetches:
        fetch.start()

    barrier = pltpu.get_barrier_semaphore()
    friends = [at(z_to=z_peers[k]) for k in range(1, NZ)] + [at(x_to=x_peers[k]) for k in range(1, NX)]
    friends += [at(y_to=y_to[way]) for y_to in (y_next, y_after) for way in range(2)]
    friends += [at(core_to=1 - core), at(zh_to=1 - zh)]
    for friend in friends:
        pl.semaphore_signal(barrier, inc=1, device_id=friend, device_id_type=MESH)

    diagonal[...] = jnp.zeros_like(diagonal)
    for fetch in fetches[:6]:
        fetch.wait()
    rank = basis_ref.shape[2]
    for number in range(4):
        diagonal[number * rank : (number + 1) * rank, number * HD : (number + 1) * HD] = basis_ref[number // 2, number % 2]
    maps = diagonal[...]
    shared = jnp.concatenate([pk_ref[...], pv_ref[...]], axis=1)
    fresh = [jnp.concatenate([nk_ref[step], nv_ref[step]], axis=1) for step in range(2)]
    mapped = nt_dot(jnp.concatenate([*fresh, shared], axis=0), maps)
    shared_mapped = mapped[2 * rows :]
    for step in range(2):
        coefficients = (mapped[step * rows : (step + 1) * rows] - shared_mapped).astype(jnp.bfloat16)
        shared = (shared.astype(jnp.float32) + nn_dot(coefficients, maps)).astype(jnp.bfloat16)
        if step == 0:
            shared_mapped = nt_dot(shared, maps)
        for number in range(4):
            zsend[2 * (number % 2) + step, number // 2] = shared[:, number * HD : (number + 1) * HD]
    for head in range(2):
        for step in range(2):
            zsend[2 * head + step, 2] = q_ref[step, :, head * HD : (head + 1) * HD]


    pl.semaphore_wait(barrier, len(friends))

    started = []

    def send(src, dst, send_sem, recv_sem, device):
        copy = pltpu.make_async_remote_copy(
            src_ref=src, dst_ref=dst, send_sem=send_sem, recv_sem=recv_sem, device_id=device, device_id_type=MESH
        )
        copy.start()
        started.append(copy)
        return copy

    z_copies, q_copies = {}, {}
    for k in range(1, NZ):
        z_copies[k] = send(
            zsend.at[z_peers[k], pl.ds(0, 2)], kv.at[0, 0, k], zs_sem.at[k], zr_sem.at[k], at(z_to=z_peers[k])
        )
    w_copies = {}
    for k in (2, 1, 3):
        for which in range(2):
            w_copies[k, which] = send(
                w_hbm.at[core_rows, columns_of(which, x_peers[k])], w_ref.at[which, x, core_rows],
                ws_sem.at[k, which], wr_sem.at[k, which], at(x_to=x_peers[k]),
            )
    kv[0, 0, 0] = zsend[z, 0:2]
    qbuf[0] = zsend[z, 2]

    ring, share, far_other = {}, {}, {}

    def push(way, distance, chunk, step):
        piece = pl.ds(chunk * PER, PER)
        ring[way, distance + step, chunk] = send(
            kv.at[0, slot_of(way, distance), piece],
            kv.at[0, slot_of(way, distance + step), piece],
            rs_sem.at[way, distance + step - 1, chunk],
            rr_sem.at[way, distance + step - 1, chunk],
            at(y_to=(y_next if step == 1 else y_after)[way]),
        )

    def far_push(way, chunk):
        push(way, HALF - 2, chunk, 2)
        piece = pl.ds(chunk * PER, PER)
        far_other[chunk] = send(
            kv.at[0, slot_of(way, HALF - 2), piece], kv.at[1, slot_of(0, HALF), piece],
            fs_sem.at[chunk], fr_sem.at[chunk], at(y_to=y_after[way], core_to=1 - core),
        )

    def share_core(way, distance, chunk):
        parts = 1 if distance < HALF - 1 else 2
        count = CHUNKS // parts
        if (chunk + 1) % count:
            return
        part = chunk // count
        piece = pl.ds(part * count * PER, count * PER)
        slot = slot_of(way, distance)
        share[slot, part] = send(
            kv.at[0, slot, piece],
            kv.at[1, slot, piece],
            cs_sem.at[slot, part],
            cr_sem.at[slot, part],
            at(core_to=1 - core),
        )

    lag = 2
    for chunk in range(CHUNKS + lag):
        if chunk < CHUNKS:
            for k in range(chunk * PER, (chunk + 1) * PER):
                if k:
                    z_copies[k].wait_recv()
            for way in range(2):
                push(way, 0, chunk, 2)
            share_core(0, 0, chunk)
        if chunk >= lag:
            for way in range(2):
                push(way, 0, chunk - lag, 1)
        if chunk == 0:
            for k in range(1, NZ):
                q_copies[k] = send(
                    zsend.at[z_peers[k], 2], qbuf.at[k], qs_sem.at[k], qr_sem.at[k], at(z_to=z_peers[k])
                )
    for k in range(1, NZ):
        q_copies[k].wait_recv()
    queries = qbuf[...].reshape(NZ * rows, HD)
    scale = HD ** (-0.5)
    block = NZ * rows
    lane_max = {}

    def group_of(distance):
        return int(distance >= HALF - 1)

    def score(side, distance):
        first, last = slot_of(0, distance), slot_of(1, distance)
        count = last - first + 1
        keys = kv[side, first : last + 1, :, 0].reshape(count * block, HD)
        begin = (side * NY + first) * block
        found = nt_dot(queries, keys) * scale
        scores[:, begin : begin + count * block] = found
        for number in range(count):
            piece = found[:, number * block : (number + 1) * block]
            group = group_of(distance)
            lane_max[group] = jnp.maximum(lane_max[group], piece) if group in lane_max else piece

    def score_other(distance):
        for slot in sorted({slot_of(0, distance), slot_of(1, distance)}):
            for part in range(2):
                if (slot, part) in share:
                    share[slot, part].wait_recv()
        for chunk in range(CHUNKS if distance == HALF else 0):
            far_other[chunk].wait_recv()
        score(1, distance)

    score(0, 0)
    for chunk in range(CHUNKS):
        for way in range(2):
            ring[way, HALF - 2, chunk].wait_recv()
            push(way, HALF - 2, chunk, 1)
        far_push(far_way(chunk), chunk)
        for way in range(2):
            share_core(way, HALF - 2, chunk)
    for chunk in range(CHUNKS):
        for way in range(2):
            ring[way, 1, chunk].wait_recv()
            share_core(way, 1, chunk)
    score(0, 2)
    score(0, 1)
    score_other(0)
    def weigh(group, row_max):
        slots = [slot_of(way, distance) for distance in range(HALF + 1) for way in range(2) if group_of(distance) == group]
        first, last = min(slots), max(slots)
        count = last - first + 1
        lane_total = jnp.zeros((block, block), jnp.float32)
        summed = jnp.zeros((block, HD), jnp.float32)
        for side in range(2):
            begin = (side * NY + first) * block
            for number in range(count):
                span = slice(begin + number * block, begin + (number + 1) * block)
                exponent = jnp.exp(scores[:, span] - row_max)
                lane_total = lane_total + exponent
                weights[:, span] = exponent.astype(jnp.bfloat16)
            values = kv[side, first : last + 1, :, 1].reshape(count * block, HD)
            summed = summed + nn_dot(weights[:, begin : begin + count * block], values)
        return lane_total, summed

    def share_last():
        for chunk in range(CHUNKS):
            for way in range(2):
                ring[way, HALF - 1, chunk].wait_recv()
                share_core(way, HALF - 1, chunk)

    score_other(2)
    score_other(1)
    near_max = jnp.max(lane_max[0], axis=1, keepdims=True)
    near_total, near_summed = weigh(0, near_max)
    share_last()
    score(0, HALF - 1)
    for chunk in range(CHUNKS):
        ring[far_way(chunk), HALF, chunk].wait_recv()
    score(0, HALF)
    score_other(HALF)
    score_other(HALF - 1)

    row_max = jnp.maximum(near_max, jnp.max(lane_max[1], axis=1, keepdims=True))
    rescale = jnp.exp(near_max - row_max)
    far_total, far_summed = weigh(1, row_max)
    row_total = jnp.sum(near_total * rescale + far_total, axis=1, keepdims=True)
    attended = ((near_summed * rescale + far_summed) / row_total).astype(jnp.bfloat16)
    asend[...] = attended.reshape(NZ, rows, HD)

    earlier = list(started)
    a_copies = {}
    for j in (2, 1, 3, 0):
        for k in (2, 1, 3, 0):
            if k or j:
                a_copies[k, j] = send(
                    asend.at[k], abuf.at[x, z], as_sem.at[k, j], ar_sem.at[k, j], at(z_to=z_back[k], x_to=x_peers[j])
                )
    abuf[x, z] = asend[0]

    v_copies = {}
    for which in range(2):
        for k in (1, 3, 2):
            w_copies[k, which].wait_recv()
            there = w_ref.at[which, x_back[k], core_rows]
            v_copies[k, which] = send(there, there, vs_sem.at[k, which], vr_sem.at[k, which], at(core_to=1 - core))
    for fetch in fetches[6:]:
        fetch.wait()
    for copy in earlier:
        copy.wait_send()
    for copy in a_copies.values():
        copy.wait_recv()
    by_step = [
        jnp.concatenate([abuf[j, 2 * head + step] for j in range(NX) for head in range(2)], axis=1) for step in range(2)
    ]
    features = jnp.concatenate(by_step, axis=0)

    def partial(which):
        for k in range(1, NX):
            v_copies[k, which].wait_recv()
        found = nn_dot(features, w_ref[which].reshape(NX * w_rows, columns))
        return found.reshape(2, rows, columns)

    there = partial(0)
    hsend[...] = there.astype(jnp.bfloat16)
    h_copies = []
    for step in range(2):
        h_copies.append(send(hsend.at[step], hrecv.at[step], hs_sem.at[step], hr_sem.at[step], at(zh_to=1 - zh)))
    here = partial(1)
    for copy in [*a_copies.values(), *v_copies.values()]:
        copy.wait_send()
    for step in range(2):
        h_copies[step].wait_recv()
        out_ref[step] = here[step] + hrecv[step].astype(jnp.float32)
    for copy in h_copies:
        copy.wait_send()


def per_device(queries, new_keys, new_values, prev_keys, prev_values, kv_basis, out_weight, out_gate):
    steps, rows, _ = queries.shape
    columns = out_gate.shape[1]
    bf16, f32 = jnp.bfloat16, jnp.float32
    vmem = pl.BlockSpec(memory_space=pltpu.VMEM)
    dma = pltpu.SemaphoreType.DMA
    tokens = 2 * NY * NZ * rows
    operands = (
        queries, new_keys, new_values, prev_keys, prev_values, jnp.swapaxes(kv_basis, 2, 3), out_weight,
    )
    summed = pl.pallas_call(
        kernel,
        out_shape=jax.ShapeDtypeStruct((steps, rows, columns), f32),
        in_specs=[pl.BlockSpec(memory_space=pltpu.HBM)] * 7,
        out_specs=vmem,
        scratch_shapes=[
            *[pltpu.VMEM(operand.shape, bf16) for operand in operands[:6]],
            pltpu.VMEM((2, NX, out_weight.shape[0], columns), bf16),
            pltpu.VMEM((4 * kv_basis.shape[3], 4 * HD), bf16),
            pltpu.VMEM((NZ, 3, rows, HD), bf16),
            pltpu.VMEM((2, NY, NZ, 2, rows, HD), bf16),
            pltpu.VMEM((NZ, rows, HD), bf16),
            pltpu.VMEM((NZ * rows, tokens), f32),
            pltpu.VMEM((NZ * rows, tokens), bf16),
            pltpu.VMEM((NZ, rows, HD), bf16),
            pltpu.VMEM((NX, NZ, rows, HD), bf16),
            pltpu.VMEM((steps, rows, columns), bf16),
            pltpu.VMEM((steps, rows, columns), bf16),
            dma((8,)),
            dma((NZ,)), dma((NZ,)), dma((NZ,)), dma((NZ,)),
            dma((2, HALF, CHUNKS)), dma((2, HALF, CHUNKS)),
            dma((NY, 2)), dma((NY, 2)),
            dma((CHUNKS,)), dma((CHUNKS,)),
            dma((NZ, NX)), dma((NZ, NX)),
            dma((NX, 2)), dma((NX, 2)), dma((NX, 2)), dma((NX, 2)),
            dma((2,)), dma((2,)),
        ],
        compiler_params=pltpu.CompilerParams(
            collective_id=0, has_side_effects=True, vmem_limit_bytes=32 * 1024 * 1024
        ),
    )(*[pltpu.with_memory_space_constraint(operand, pltpu.HBM) for operand in operands])
    return (out_gate[:, None, :] * summed).astype(bf16)


def solution(mesh):
    placed = (
        P(None, "patch", "tp"),
        P(None, "patch", "tp"),
        P(None, "patch", "tp"),
        P("patch", "tp"),
        P("patch", "tp"),
        P(None, "tp", None, None),
        P("tp", None),
        P(None, "tp"),
    )
    return jax.shard_map(
        per_device, mesh=mesh, in_specs=placed, out_specs=P(None, "patch", "tp"), check_vma=False
    )
```

```python
import functools

import jax
import jax.numpy as jnp
from jax import lax
from jax.experimental import pallas as pl
from jax.experimental.pallas import tpu as pltpu
from jax.sharding import PartitionSpec as P

MESH = pl.DeviceIdType.MESH
NZ = 4
NY = 8
NX = 4
HD = 128
CHUNKS = 2
PER = NZ // CHUNKS
HALF = NY // 2


def slot_of(way, distance):
    if distance == 0 or distance == HALF:
        return 2 * distance - (distance == HALF)
    return 2 * distance - 1 + way


def far_way(chunk):
    return 0 if chunk < CHUNKS // 2 else 1


def nt_dot(a, b):
    return lax.dot_general(a, b, (((1,), (1,)), ((), ())), preferred_element_type=jnp.float32)


def nn_dot(a, b):
    return jnp.dot(a, b, preferred_element_type=jnp.float32)


def kernel(
    q_hbm, nk_hbm, nv_hbm, pk_hbm, pv_hbm, basis_hbm, w_hbm, out_ref,
    q_ref, nk_ref, nv_ref, pk_ref, pv_ref, basis_ref, w_ref,
    diagonal, zsend, kv, qbuf, scores, weights, asend, abuf, hsend, hrecv,
    in_sem, zs_sem, zr_sem, qs_sem, qr_sem, rs_sem, rr_sem, cs_sem, cr_sem,
    fs_sem, fr_sem, as_sem, ar_sem, ws_sem, wr_sem, vs_sem, vr_sem, hs_sem, hr_sem,
):
    rows = pk_ref.shape[0]
    columns = out_ref.shape[2]
    patch, tp = lax.axis_index("patch"), lax.axis_index("tp")
    core = patch % 2
    y = (patch // 2) % NY
    z = patch // (2 * NY)
    x = tp % NX
    zh = tp // NX

    def at(z_to=None, y_to=None, core_to=None, x_to=None, zh_to=None):
        z_t = z if z_to is None else z_to
        y_t = y if y_to is None else y_to
        c_t = core if core_to is None else core_to
        x_t = x if x_to is None else x_to
        h_t = zh if zh_to is None else zh_to
        return ((z_t * NY + y_t) * 2 + c_t, h_t * NX + x_t)

    z_peers = [lax.rem(z + k, NZ) for k in range(NZ)]
    z_back = [lax.rem(z + NZ - k, NZ) for k in range(NZ)]
    x_peers = [lax.rem(x + k, NX) for k in range(NX)]
    x_back = [lax.rem(x + NX - k, NX) for k in range(NX)]
    y_next = [lax.rem(y + 1, NY), lax.rem(y + NY - 1, NY)]
    y_after = [lax.rem(y + 2, NY), lax.rem(y + NY - 2, NY)]

    halves = (1 - zh, zh)
    w_rows = w_hbm.shape[0]
    core_rows = pl.ds(pl.multiple_of(core * (w_rows // 2), w_rows // 2), w_rows // 2)

    def columns_of(which, x_to):
        return pl.ds(pl.multiple_of((halves[which] * NX + x_to) * columns, columns), columns)

    fetches = [
        pltpu.make_async_copy(source, target, in_sem.at[number])
        for number, (source, target) in enumerate(
            (
                (basis_hbm, basis_ref), (nk_hbm, nk_ref), (pk_hbm, pk_ref), (nv_hbm, nv_ref),
                (pv_hbm, pv_ref), (q_hbm, q_ref),
                (w_hbm.at[:, columns_of(0, x)], w_ref.at[0, x]), (w_hbm.at[:, columns_of(1, x)], w_ref.at[1, x]),
            )
        )
    ]
    for fetch in fetches[:5]:
        fetch.start()

    barrier = pltpu.get_barrier_semaphore()
    friends = [at(z_to=z_peers[k]) for k in range(1, NZ)] + [at(x_to=x_peers[k]) for k in range(1, NX)]
    friends += [at(y_to=y_to[way]) for y_to in (y_next, y_after) for way in range(2)]
    friends += [at(core_to=1 - core), at(zh_to=1 - zh)]
    for friend in friends:
        pl.semaphore_signal(barrier, inc=1, device_id=friend, device_id_type=MESH)

    for fetch in fetches[5:]:
        fetch.start()
    diagonal[...] = jnp.zeros_like(diagonal)
    for fetch in fetches[:5]:
        fetch.wait()

    def z_copy(pair, k):
        return pltpu.make_async_remote_copy(
            src_ref=zsend.at[pair, pl.ds(0, 2)], dst_ref=kv.at[0, 0, k],
            send_sem=zs_sem.at[k], recv_sem=zr_sem.at[k], device_id=at(z_to=pair), device_id_type=MESH,
        )

    def send_pair(pair):
        @pl.when(z != pair)
        def _():
            z_copy(pair, lax.rem(pair - z + NZ, NZ)).start()

    rank = basis_ref.shape[2]
    for number in range(4):
        diagonal[number * rank : (number + 1) * rank, number * HD : (number + 1) * HD] = basis_ref[number // 2, number % 2]
    maps = diagonal[...]
    shared = jnp.concatenate([pk_ref[...], pv_ref[...]], axis=1)
    fresh = [jnp.concatenate([nk_ref[step], nv_ref[step]], axis=1) for step in range(2)]
    mapped = nt_dot(jnp.concatenate([*fresh, shared], axis=0), maps)
    shared_mapped = mapped[2 * rows :]
    for step in range(2):
        coefficients = (mapped[step * rows : (step + 1) * rows] - shared_mapped).astype(jnp.bfloat16)
        shared = (shared.astype(jnp.float32) + nn_dot(coefficients, maps)).astype(jnp.bfloat16)
        if step == 0:
            shared_mapped = nt_dot(shared, maps)
        for number in range(4):
            zsend[2 * (number % 2) + step, number // 2] = shared[:, number * HD : (number + 1) * HD]
        if step == 0:
            pl.semaphore_wait(barrier, len(friends))
        for head in range(2):
            send_pair(2 * head + step)

    started = []

    def send(src, dst, send_sem, recv_sem, device):
        copy = pltpu.make_async_remote_copy(
            src_ref=src, dst_ref=dst, send_sem=send_sem, recv_sem=recv_sem, device_id=device, device_id_type=MESH
        )
        copy.start()
        started.append(copy)
        return copy

    z_copies, q_copies = {}, {}
    for k in range(1, NZ):
        z_copies[k] = z_copy(z_peers[k], k)
        started.append(z_copies[k])
    kv[0, 0, 0] = zsend[z, 0:2]
    fetches[5].wait()
    for head in range(2):
        for step in range(2):
            zsend[2 * head + step, 2] = q_ref[step, :, head * HD : (head + 1) * HD]
    w_copies = {}
    for k in (2, 1, 3):
        for which in range(2):
            w_copies[k, which] = send(
                w_hbm.at[core_rows, columns_of(which, x_peers[k])], w_ref.at[which, x, core_rows],
                ws_sem.at[k, which], wr_sem.at[k, which], at(x_to=x_peers[k]),
            )
    qbuf[0] = zsend[z, 2]

    ring, share, far_other = {}, {}, {}

    def push(way, distance, chunk, step):
        piece = pl.ds(chunk * PER, PER)
        ring[way, distance + step, chunk] = send(
            kv.at[0, slot_of(way, distance), piece],
            kv.at[0, slot_of(way, distance + step), piece],
            rs_sem.at[way, distance + step - 1, chunk],
            rr_sem.at[way, distance + step - 1, chunk],
            at(y_to=(y_next if step == 1 else y_after)[way]),
        )

    def far_push(way, chunk):
        push(way, HALF - 2, chunk, 2)
        piece = pl.ds(chunk * PER, PER)
        far_other[chunk] = send(
            kv.at[0, slot_of(way, HALF - 2), piece], kv.at[1, slot_of(0, HALF), piece],
            fs_sem.at[chunk], fr_sem.at[chunk], at(y_to=y_after[way], core_to=1 - core),
        )

    def share_core(way, distance, chunk):
        parts = 1 if distance < HALF - 1 else 2
        count = CHUNKS // parts
        if (chunk + 1) % count:
            return
        part = chunk // count
        piece = pl.ds(part * count * PER, count * PER)
        slot = slot_of(way, distance)
        share[slot, part] = send(
            kv.at[0, slot, piece],
            kv.at[1, slot, piece],
            cs_sem.at[slot, part],
            cr_sem.at[slot, part],
            at(core_to=1 - core),
        )

    lag = 2
    for chunk in range(CHUNKS + lag):
        if chunk < CHUNKS:
            for k in range(chunk * PER, (chunk + 1) * PER):
                if k:
                    z_copies[k].wait_recv()
            for way in range(2):
                push(way, 0, chunk, 2)
            share_core(0, 0, chunk)
        if chunk >= lag:
            for way in range(2):
                push(way, 0, chunk - lag, 1)
        if chunk == 0:
            for k in range(1, NZ):
                q_copies[k] = send(
                    zsend.at[z_peers[k], 2], qbuf.at[k], qs_sem.at[k], qr_sem.at[k], at(z_to=z_peers[k])
                )
    for k in range(1, NZ):
        q_copies[k].wait_recv()
    queries = qbuf[...].reshape(NZ * rows, HD)
    scale = HD ** (-0.5)
    block = NZ * rows
    lane_max = {}

    def group_of(distance):
        return int(distance >= HALF - 1)

    def score(side, distance):
        first, last = slot_of(0, distance), slot_of(1, distance)
        count = last - first + 1
        keys = kv[side, first : last + 1, :, 0].reshape(count * block, HD)
        begin = (side * NY + first) * block
        found = nt_dot(queries, keys) * scale
        scores[:, begin : begin + count * block] = found
        for number in range(count):
            piece = found[:, number * block : (number + 1) * block]
            group = group_of(distance)
            lane_max[group] = jnp.maximum(lane_max[group], piece) if group in lane_max else piece

    def score_other(distance):
        for slot in sorted({slot_of(0, distance), slot_of(1, distance)}):
            for part in range(2):
                if (slot, part) in share:
                    share[slot, part].wait_recv()
        for chunk in range(CHUNKS if distance == HALF else 0):
            far_other[chunk].wait_recv()
        score(1, distance)

    score(0, 0)
    for chunk in range(CHUNKS):
        for way in range(2):
            ring[way, HALF - 2, chunk].wait_recv()
            push(way, HALF - 2, chunk, 1)
        far_push(far_way(chunk), chunk)
        for way in range(2):
            share_core(way, HALF - 2, chunk)
    for chunk in range(CHUNKS):
        for way in range(2):
            ring[way, 1, chunk].wait_recv()
            share_core(way, 1, chunk)
    score(0, 2)
    score(0, 1)
    score_other(0)
    def weigh(group, row_max):
        slots = [slot_of(way, distance) for distance in range(HALF + 1) for way in range(2) if group_of(distance) == group]
        first, last = min(slots), max(slots)
        count = last - first + 1
        lane_total = jnp.zeros((block, block), jnp.float32)
        summed = jnp.zeros((block, HD), jnp.float32)
        for side in range(2):
            begin = (side * NY + first) * block
            for number in range(count):
                span = slice(begin + number * block, begin + (number + 1) * block)
                exponent = jnp.exp(scores[:, span] - row_max)
                lane_total = lane_total + exponent
                weights[:, span] = exponent.astype(jnp.bfloat16)
            values = kv[side, first : last + 1, :, 1].reshape(count * block, HD)
            summed = summed + nn_dot(weights[:, begin : begin + count * block], values)
        return lane_total, summed

    def share_last():
        for chunk in range(CHUNKS):
            for way in range(2):
                ring[way, HALF - 1, chunk].wait_recv()
                share_core(way, HALF - 1, chunk)

    score_other(2)
    score_other(1)
    near_max = jnp.max(lane_max[0], axis=1, keepdims=True)
    near_total, near_summed = weigh(0, near_max)
    share_last()
    score(0, HALF - 1)
    for chunk in range(CHUNKS):
        ring[far_way(chunk), HALF, chunk].wait_recv()
    score(0, HALF)
    score_other(HALF)
    score_other(HALF - 1)

    row_max = jnp.maximum(near_max, jnp.max(lane_max[1], axis=1, keepdims=True))
    rescale = jnp.exp(near_max - row_max)
    far_total, far_summed = weigh(1, row_max)
    row_total = jnp.sum(near_total * rescale + far_total, axis=1, keepdims=True)
    attended = ((near_summed * rescale + far_summed) / row_total).astype(jnp.bfloat16)
    asend[...] = attended.reshape(NZ, rows, HD)

    earlier = list(started)
    a_copies = {}
    for j in (2, 1, 3, 0):
        for k in (2, 1, 3, 0):
            if k or j:
                a_copies[k, j] = send(
                    asend.at[k], abuf.at[x, z], as_sem.at[k, j], ar_sem.at[k, j], at(z_to=z_back[k], x_to=x_peers[j])
                )
    abuf[x, z] = asend[0]

    v_copies = {}
    for which in range(2):
        for k in (1, 3, 2):
            w_copies[k, which].wait_recv()
            there = w_ref.at[which, x_back[k], core_rows]
            v_copies[k, which] = send(there, there, vs_sem.at[k, which], vr_sem.at[k, which], at(core_to=1 - core))
    for fetch in fetches[6:]:
        fetch.wait()
    for copy in earlier:
        copy.wait_send()
    for copy in a_copies.values():
        copy.wait_recv()
    by_step = [
        jnp.concatenate([abuf[j, 2 * head + step] for j in range(NX) for head in range(2)], axis=1) for step in range(2)
    ]
    features = jnp.concatenate(by_step, axis=0)

    def partial(which):
        for k in range(1, NX):
            v_copies[k, which].wait_recv()
        found = nn_dot(features, w_ref[which].reshape(NX * w_rows, columns))
        return found.reshape(2, rows, columns)

    there = partial(0)
    hsend[...] = there.astype(jnp.bfloat16)
    h_copies = []
    for step in range(2):
        h_copies.append(send(hsend.at[step], hrecv.at[step], hs_sem.at[step], hr_sem.at[step], at(zh_to=1 - zh)))
    here = partial(1)
    for copy in [*a_copies.values(), *v_copies.values()]:
        copy.wait_send()
    for step in range(2):
        h_copies[step].wait_recv()
        out_ref[step] = here[step] + hrecv[step].astype(jnp.float32)
    for copy in h_copies:
        copy.wait_send()


def per_device(queries, new_keys, new_values, prev_keys, prev_values, kv_basis, out_weight, out_gate):
    steps, rows, _ = queries.shape
    columns = out_gate.shape[1]
    bf16, f32 = jnp.bfloat16, jnp.float32
    vmem = pl.BlockSpec(memory_space=pltpu.VMEM)
    dma = pltpu.SemaphoreType.DMA
    tokens = 2 * NY * NZ * rows
    operands = (
        queries, new_keys, new_values, prev_keys, prev_values, jnp.swapaxes(kv_basis, 2, 3), out_weight,
    )
    summed = pl.pallas_call(
        kernel,
        out_shape=jax.ShapeDtypeStruct((steps, rows, columns), f32),
        in_specs=[pl.BlockSpec(memory_space=pltpu.HBM)] * 7,
        out_specs=vmem,
        scratch_shapes=[
            *[pltpu.VMEM(operand.shape, bf16) for operand in operands[:6]],
            pltpu.VMEM((2, NX, out_weight.shape[0], columns), bf16),
            pltpu.VMEM((4 * kv_basis.shape[3], 4 * HD), bf16),
            pltpu.VMEM((NZ, 3, rows, HD), bf16),
            pltpu.VMEM((2, NY, NZ, 2, rows, HD), bf16),
            pltpu.VMEM((NZ, rows, HD), bf16),
            pltpu.VMEM((NZ * rows, tokens), f32),
            pltpu.VMEM((NZ * rows, tokens), bf16),
            pltpu.VMEM((NZ, rows, HD), bf16),
            pltpu.VMEM((NX, NZ, rows, HD), bf16),
            pltpu.VMEM((steps, rows, columns), bf16),
            pltpu.VMEM((steps, rows, columns), bf16),
            dma((8,)),
            dma((NZ,)), dma((NZ,)), dma((NZ,)), dma((NZ,)),
            dma((2, HALF, CHUNKS)), dma((2, HALF, CHUNKS)),
            dma((NY, 2)), dma((NY, 2)),
            dma((CHUNKS,)), dma((CHUNKS,)),
            dma((NZ, NX)), dma((NZ, NX)),
            dma((NX, 2)), dma((NX, 2)), dma((NX, 2)), dma((NX, 2)),
            dma((2,)), dma((2,)),
        ],
        compiler_params=pltpu.CompilerParams(
            collective_id=0, has_side_effects=True, vmem_limit_bytes=32 * 1024 * 1024
        ),
    )(*[pltpu.with_memory_space_constraint(operand, pltpu.HBM) for operand in operands])
    return (out_gate[:, None, :] * summed).astype(bf16)


def solution(mesh):
    placed = (
        P(None, "patch", "tp"),
        P(None, "patch", "tp"),
        P(None, "patch", "tp"),
        P("patch", "tp"),
        P("patch", "tp"),
        P(None, "tp", None, None),
        P("tp", None),
        P(None, "tp"),
    )
    return jax.shard_map(
        per_device, mesh=mesh, in_specs=placed, out_specs=P(None, "patch", "tp"), check_vma=False
    )
```

```python
import functools

import jax
import jax.numpy as jnp
from jax import lax
from jax.experimental import pallas as pl
from jax.experimental.pallas import tpu as pltpu
from jax.sharding import PartitionSpec as P

MESH = pl.DeviceIdType.MESH
NZ = 4
NY = 8
NX = 4
HD = 128
CHUNKS = 2
PER = NZ // CHUNKS
HALF = NY // 2


def slot_of(way, distance):
    if distance == 0 or distance == HALF:
        return 2 * distance - (distance == HALF)
    return 2 * distance - 1 + way


def far_way(chunk):
    return 0 if chunk < CHUNKS // 2 else 1


def nt_dot(a, b):
    return lax.dot_general(a, b, (((1,), (1,)), ((), ())), preferred_element_type=jnp.float32)


def nn_dot(a, b):
    return jnp.dot(a, b, preferred_element_type=jnp.float32)


def kernel(
    q_hbm, nk_hbm, nv_hbm, pk_hbm, pv_hbm, basis_hbm, w_hbm, out_ref,
    q_ref, nk_ref, nv_ref, pk_ref, pv_ref, basis_ref, w_ref,
    diagonal, zsend, kv, qbuf, scores, weights, asend, abuf, hsend, hrecv,
    in_sem, zs_sem, zr_sem, qs_sem, qr_sem, rs_sem, rr_sem, cs_sem, cr_sem,
    fs_sem, fr_sem, as_sem, ar_sem, ws_sem, wr_sem, vs_sem, vr_sem, hs_sem, hr_sem,
):
    rows = pk_ref.shape[0]
    columns = out_ref.shape[2]
    patch, tp = lax.axis_index("patch"), lax.axis_index("tp")
    core = patch % 2
    y = (patch // 2) % NY
    z = patch // (2 * NY)
    x = tp % NX
    zh = tp // NX

    def at(z_to=None, y_to=None, core_to=None, x_to=None, zh_to=None):
        z_t = z if z_to is None else z_to
        y_t = y if y_to is None else y_to
        c_t = core if core_to is None else core_to
        x_t = x if x_to is None else x_to
        h_t = zh if zh_to is None else zh_to
        return ((z_t * NY + y_t) * 2 + c_t, h_t * NX + x_t)

    z_peers = [lax.rem(z + k, NZ) for k in range(NZ)]
    z_back = [lax.rem(z + NZ - k, NZ) for k in range(NZ)]
    x_peers = [lax.rem(x + k, NX) for k in range(NX)]
    x_back = [lax.rem(x + NX - k, NX) for k in range(NX)]
    y_next = [lax.rem(y + 1, NY), lax.rem(y + NY - 1, NY)]
    y_after = [lax.rem(y + 2, NY), lax.rem(y + NY - 2, NY)]

    halves = (1 - zh, zh)
    w_rows = w_hbm.shape[0]
    core_rows = pl.ds(pl.multiple_of(core * (w_rows // 2), w_rows // 2), w_rows // 2)

    def columns_of(which, x_to):
        return pl.ds(pl.multiple_of((halves[which] * NX + x_to) * columns, columns), columns)

    fetches = [
        pltpu.make_async_copy(source, target, in_sem.at[number])
        for number, (source, target) in enumerate(
            (
                (basis_hbm, basis_ref), (nk_hbm, nk_ref), (pk_hbm, pk_ref), (nv_hbm, nv_ref),
                (pv_hbm, pv_ref), (q_hbm, q_ref),
                (w_hbm.at[:, columns_of(0, x)], w_ref.at[0, x]), (w_hbm.at[:, columns_of(1, x)], w_ref.at[1, x]),
            )
        )
    ]
    for fetch in fetches[:5]:
        fetch.start()

    barrier = pltpu.get_barrier_semaphore()
    friends = [at(z_to=z_peers[k]) for k in range(1, NZ)] + [at(x_to=x_peers[k]) for k in range(1, NX)]
    friends += [at(y_to=y_to[way]) for y_to in (y_next, y_after) for way in range(2)]
    friends += [at(core_to=1 - core), at(zh_to=1 - zh)]
    for friend in friends:
        pl.semaphore_signal(barrier, inc=1, device_id=friend, device_id_type=MESH)

    for fetch in fetches[5:]:
        fetch.start()
    diagonal[...] = jnp.zeros_like(diagonal)
    for fetch in fetches[:5]:
        fetch.wait()

    def z_copy(pair, k):
        return pltpu.make_async_remote_copy(
            src_ref=zsend.at[pair, pl.ds(0, 2)], dst_ref=kv.at[0, 0, k],
            send_sem=zs_sem.at[k], recv_sem=zr_sem.at[k], device_id=at(z_to=pair), device_id_type=MESH,
        )

    def send_pair(pair):
        @pl.when(z != pair)
        def _():
            z_copy(pair, lax.rem(pair - z + NZ, NZ)).start()

    rank = basis_ref.shape[2]
    for number in range(4):
        diagonal[number * rank : (number + 1) * rank, number * HD : (number + 1) * HD] = basis_ref[number // 2, number % 2]
    maps = diagonal[...]
    shared = jnp.concatenate([pk_ref[...], pv_ref[...]], axis=1)
    fresh = [jnp.concatenate([nk_ref[step], nv_ref[step]], axis=1) for step in range(2)]
    mapped = nt_dot(jnp.concatenate([*fresh, shared], axis=0), maps)
    shared_mapped = mapped[2 * rows :]
    for step in range(2):
        coefficients = (mapped[step * rows : (step + 1) * rows] - shared_mapped).astype(jnp.bfloat16)
        shared = (shared.astype(jnp.float32) + nn_dot(coefficients, maps)).astype(jnp.bfloat16)
        if step == 0:
            shared_mapped = nt_dot(shared, maps)
        for number in range(4):
            zsend[2 * (number % 2) + step, number // 2] = shared[:, number * HD : (number + 1) * HD]
        if step == 0:
            pl.semaphore_wait(barrier, len(friends))
        for head in range(2):
            send_pair(2 * head + step)

    started = []

    def send(src, dst, send_sem, recv_sem, device):
        copy = pltpu.make_async_remote_copy(
            src_ref=src, dst_ref=dst, send_sem=send_sem, recv_sem=recv_sem, device_id=device, device_id_type=MESH
        )
        copy.start()
        started.append(copy)
        return copy

    z_copies, q_copies = {}, {}
    for k in range(1, NZ):
        z_copies[k] = z_copy(z_peers[k], k)
        started.append(z_copies[k])
    kv[0, 0, 0] = zsend[z, 0:2]
    fetches[5].wait()
    for head in range(2):
        for step in range(2):
            zsend[2 * head + step, 2] = q_ref[step, :, head * HD : (head + 1) * HD]
    w_copies = {}
    for k in (2, 1, 3):
        for which in range(2):
            w_copies[k, which] = send(
                w_hbm.at[core_rows, columns_of(which, x_peers[k])], w_ref.at[which, x, core_rows],
                ws_sem.at[k, which], wr_sem.at[k, which], at(x_to=x_peers[k]),
            )
    qbuf[0] = zsend[z, 2]

    ring, share, far_other = {}, {}, {}

    def push(way, distance, chunk, step):
        piece = pl.ds(chunk * PER, PER)
        ring[way, distance + step, chunk] = send(
            kv.at[0, slot_of(way, distance), piece],
            kv.at[0, slot_of(way, distance + step), piece],
            rs_sem.at[way, distance + step - 1, chunk],
            rr_sem.at[way, distance + step - 1, chunk],
            at(y_to=(y_next if step == 1 else y_after)[way]),
        )

    def far_push(way, chunk):
        push(way, HALF - 2, chunk, 2)
        piece = pl.ds(chunk * PER, PER)
        far_other[chunk] = send(
            kv.at[0, slot_of(way, HALF - 2), piece], kv.at[1, slot_of(0, HALF), piece],
            fs_sem.at[chunk], fr_sem.at[chunk], at(y_to=y_after[way], core_to=1 - core),
        )

    def share_core(way, distance, chunk):
        parts = 1 if distance < HALF - 1 else 2
        count = CHUNKS // parts
        if (chunk + 1) % count:
            return
        part = chunk // count
        piece = pl.ds(part * count * PER, count * PER)
        slot = slot_of(way, distance)
        share[slot, part] = send(
            kv.at[0, slot, piece],
            kv.at[1, slot, piece],
            cs_sem.at[slot, part],
            cr_sem.at[slot, part],
            at(core_to=1 - core),
        )

    lag = 2
    for chunk in range(CHUNKS + lag):
        if chunk < CHUNKS:
            for k in range(chunk * PER, (chunk + 1) * PER):
                if k:
                    z_copies[k].wait_recv()
            for way in range(2):
                push(way, 0, chunk, 2)
            share_core(0, 0, chunk)
        if chunk >= lag:
            for way in range(2):
                push(way, 0, chunk - lag, 1)
        if chunk == 0:
            for k in range(1, NZ):
                q_copies[k] = send(
                    zsend.at[z_peers[k], 2], qbuf.at[k], qs_sem.at[k], qr_sem.at[k], at(z_to=z_peers[k])
                )
    for k in range(1, NZ):
        q_copies[k].wait_recv()
    queries = qbuf[...].reshape(NZ * rows, HD)
    scale = HD ** (-0.5)
    block = NZ * rows
    lane_max = {}

    def group_of(distance):
        return int(distance >= HALF - 1)

    def score(side, distance):
        first, last = slot_of(0, distance), slot_of(1, distance)
        count = last - first + 1
        keys = kv[side, first : last + 1, :, 0].reshape(count * block, HD)
        begin = (side * NY + first) * block
        found = nt_dot(queries, keys) * scale
        scores[:, begin : begin + count * block] = found
        for number in range(count):
            piece = found[:, number * block : (number + 1) * block]
            group = group_of(distance)
            lane_max[group] = jnp.maximum(lane_max[group], piece) if group in lane_max else piece

    def score_other(distance):
        for slot in sorted({slot_of(0, distance), slot_of(1, distance)}):
            for part in range(2):
                if (slot, part) in share:
                    share[slot, part].wait_recv()
        for chunk in range(CHUNKS if distance == HALF else 0):
            far_other[chunk].wait_recv()
        score(1, distance)

    score(0, 0)
    for chunk in range(CHUNKS):
        for way in range(2):
            ring[way, HALF - 2, chunk].wait_recv()
            push(way, HALF - 2, chunk, 1)
        far_push(far_way(chunk), chunk)
        for way in range(2):
            share_core(way, HALF - 2, chunk)
    for chunk in range(CHUNKS):
        for way in range(2):
            ring[way, 1, chunk].wait_recv()
            share_core(way, 1, chunk)
    score(0, 2)
    score(0, 1)
    score_other(0)
    def weigh(group, row_max, own_rows):
        slots = [slot_of(way, distance) for distance in range(HALF + 1) for way in range(2) if group_of(distance) == group]
        first, last = min(slots), max(slots)
        count = last - first + 1
        lane_total = jnp.zeros((row_max.shape[0], block), jnp.float32)
        summed = jnp.zeros((row_max.shape[0], HD), jnp.float32)
        for side in range(2):
            begin = (side * NY + first) * block
            for number in range(count):
                span = slice(begin + number * block, begin + (number + 1) * block)
                exponent = jnp.exp(scores[own_rows, span] - row_max)
                lane_total = lane_total + exponent
                weights[own_rows, span] = exponent.astype(jnp.bfloat16)
            values = kv[side, first : last + 1, :, 1].reshape(count * block, HD)
            summed = summed + nn_dot(weights[own_rows, begin : begin + count * block], values)
        return lane_total, summed

    def share_last():
        for chunk in range(CHUNKS):
            for way in range(2):
                ring[way, HALF - 1, chunk].wait_recv()
                share_core(way, HALF - 1, chunk)

    score_other(2)
    score_other(1)
    near_max = jnp.max(lane_max[0], axis=1, keepdims=True)
    near_total, near_summed = weigh(0, near_max, slice(0, block))
    share_last()
    score(0, HALF - 1)
    for chunk in range(CHUNKS):
        ring[far_way(chunk), HALF, chunk].wait_recv()
    score(0, HALF)
    score_other(HALF)
    score_other(HALF - 1)

    earlier = list(started)
    a_copies = {}
    part, owners = block // 2, NZ // 2
    all_max = jnp.maximum(near_max, jnp.max(lane_max[1], axis=1, keepdims=True))
    for half in (1, 0):
        own_rows = slice(half * part, (half + 1) * part)
        rescale = jnp.exp(near_max[own_rows] - all_max[own_rows])
        far_total, far_summed = weigh(1, all_max[own_rows], own_rows)
        row_total = jnp.sum(near_total[own_rows] * rescale + far_total, axis=1, keepdims=True)
        attended = ((near_summed[own_rows] * rescale + far_summed) / row_total).astype(jnp.bfloat16)
        asend[half * owners : (half + 1) * owners] = attended.reshape(owners, rows, HD)
        for j in (2, 1, 3, 0):
            for k in range(half * owners, (half + 1) * owners):
                if k or j:
                    a_copies[k, j] = send(
                        asend.at[k], abuf.at[x, z], as_sem.at[k, j], ar_sem.at[k, j], at(z_to=z_back[k], x_to=x_peers[j])
                    )
    abuf[x, z] = asend[0]

    v_copies = {}
    for which in range(2):
        for k in (1, 3, 2):
            w_copies[k, which].wait_recv()
            there = w_ref.at[which, x_back[k], core_rows]
            v_copies[k, which] = send(there, there, vs_sem.at[k, which], vr_sem.at[k, which], at(core_to=1 - core))
    for fetch in fetches[6:]:
        fetch.wait()
    for copy in earlier:
        copy.wait_send()
    for copy in a_copies.values():
        copy.wait_recv()
    by_step = [
        jnp.concatenate([abuf[j, 2 * head + step] for j in range(NX) for head in range(2)], axis=1) for step in range(2)
    ]
    features = jnp.concatenate(by_step, axis=0)

    def partial(which):
        for k in range(1, NX):
            v_copies[k, which].wait_recv()
        found = nn_dot(features, w_ref[which].reshape(NX * w_rows, columns))
        return found.reshape(2, rows, columns)

    there = partial(0)
    hsend[...] = there.astype(jnp.bfloat16)
    h_copies = []
    for step in range(2):
        h_copies.append(send(hsend.at[step], hrecv.at[step], hs_sem.at[step], hr_sem.at[step], at(zh_to=1 - zh)))
    here = partial(1)
    for copy in [*a_copies.values(), *v_copies.values()]:
        copy.wait_send()
    for step in range(2):
        h_copies[step].wait_recv()
        out_ref[step] = here[step] + hrecv[step].astype(jnp.float32)
    for copy in h_copies:
        copy.wait_send()


def per_device(queries, new_keys, new_values, prev_keys, prev_values, kv_basis, out_weight, out_gate):
    steps, rows, _ = queries.shape
    columns = out_gate.shape[1]
    bf16, f32 = jnp.bfloat16, jnp.float32
    vmem = pl.BlockSpec(memory_space=pltpu.VMEM)
    dma = pltpu.SemaphoreType.DMA
    tokens = 2 * NY * NZ * rows
    operands = (
        queries, new_keys, new_values, prev_keys, prev_values, jnp.swapaxes(kv_basis, 2, 3), out_weight,
    )
    summed = pl.pallas_call(
        kernel,
        out_shape=jax.ShapeDtypeStruct((steps, rows, columns), f32),
        in_specs=[pl.BlockSpec(memory_space=pltpu.HBM)] * 7,
        out_specs=vmem,
        scratch_shapes=[
            *[pltpu.VMEM(operand.shape, bf16) for operand in operands[:6]],
            pltpu.VMEM((2, NX, out_weight.shape[0], columns), bf16),
            pltpu.VMEM((4 * kv_basis.shape[3], 4 * HD), bf16),
            pltpu.VMEM((NZ, 3, rows, HD), bf16),
            pltpu.VMEM((2, NY, NZ, 2, rows, HD), bf16),
            pltpu.VMEM((NZ, rows, HD), bf16),
            pltpu.VMEM((NZ * rows, tokens), f32),
            pltpu.VMEM((NZ * rows, tokens), bf16),
            pltpu.VMEM((NZ, rows, HD), bf16),
            pltpu.VMEM((NX, NZ, rows, HD), bf16),
            pltpu.VMEM((steps, rows, columns), bf16),
            pltpu.VMEM((steps, rows, columns), bf16),
            dma((8,)),
            dma((NZ,)), dma((NZ,)), dma((NZ,)), dma((NZ,)),
            dma((2, HALF, CHUNKS)), dma((2, HALF, CHUNKS)),
            dma((NY, 2)), dma((NY, 2)),
            dma((CHUNKS,)), dma((CHUNKS,)),
            dma((NZ, NX)), dma((NZ, NX)),
            dma((NX, 2)), dma((NX, 2)), dma((NX, 2)), dma((NX, 2)),
            dma((2,)), dma((2,)),
        ],
        compiler_params=pltpu.CompilerParams(
            collective_id=0, has_side_effects=True, vmem_limit_bytes=32 * 1024 * 1024
        ),
    )(*[pltpu.with_memory_space_constraint(operand, pltpu.HBM) for operand in operands])
    return (out_gate[:, None, :] * summed).astype(bf16)


def solution(mesh):
    placed = (
        P(None, "patch", "tp"),
        P(None, "patch", "tp"),
        P(None, "patch", "tp"),
        P("patch", "tp"),
        P("patch", "tp"),
        P(None, "tp", None, None),
        P("tp", None),
        P(None, "tp"),
    )
    return jax.shard_map(
        per_device, mesh=mesh, in_specs=placed, out_specs=P(None, "patch", "tp"), check_vma=False
    )
```

```python
import functools

import jax
import jax.numpy as jnp
from jax import lax
from jax.experimental import pallas as pl
from jax.experimental.pallas import tpu as pltpu
from jax.sharding import PartitionSpec as P

MESH = pl.DeviceIdType.MESH
NZ = 4
NY = 8
NX = 4
HD = 128
CHUNKS = 2
PER = NZ // CHUNKS
HALF = NY // 2


def slot_of(way, distance):
    if distance == 0 or distance == HALF:
        return 2 * distance - (distance == HALF)
    return 2 * distance - 1 + way


def far_way(chunk):
    return 0 if chunk < CHUNKS // 2 else 1


def nt_dot(a, b):
    return lax.dot_general(a, b, (((1,), (1,)), ((), ())), preferred_element_type=jnp.float32)


def nn_dot(a, b):
    return jnp.dot(a, b, preferred_element_type=jnp.float32)


def kernel(
    q_hbm, nk_hbm, nv_hbm, pk_hbm, pv_hbm, basis_hbm, w_hbm, out_ref,
    q_ref, nk_ref, nv_ref, pk_ref, pv_ref, basis_ref, w_ref,
    diagonal, zsend, kv, qbuf, scores, weights, asend, abuf, hsend, hrecv,
    in_sem, zs_sem, zr_sem, qs_sem, qr_sem, rs_sem, rr_sem, cs_sem, cr_sem,
    fs_sem, fr_sem, as_sem, ar_sem, ws_sem, wr_sem, vs_sem, vr_sem, hs_sem, hr_sem,
):
    rows = pk_ref.shape[0]
    columns = out_ref.shape[2]
    patch, tp = lax.axis_index("patch"), lax.axis_index("tp")
    core = patch % 2
    y = (patch // 2) % NY
    z = patch // (2 * NY)
    x = tp % NX
    zh = tp // NX

    def at(z_to=None, y_to=None, core_to=None, x_to=None, zh_to=None):
        z_t = z if z_to is None else z_to
        y_t = y if y_to is None else y_to
        c_t = core if core_to is None else core_to
        x_t = x if x_to is None else x_to
        h_t = zh if zh_to is None else zh_to
        return ((z_t * NY + y_t) * 2 + c_t, h_t * NX + x_t)

    z_peers = [lax.rem(z + k, NZ) for k in range(NZ)]
    z_back = [lax.rem(z + NZ - k, NZ) for k in range(NZ)]
    x_peers = [lax.rem(x + k, NX) for k in range(NX)]
    x_back = [lax.rem(x + NX - k, NX) for k in range(NX)]
    y_next = [lax.rem(y + 1, NY), lax.rem(y + NY - 1, NY)]
    y_after = [lax.rem(y + 2, NY), lax.rem(y + NY - 2, NY)]

    halves = (1 - zh, zh)
    w_rows = w_hbm.shape[0]
    core_rows = pl.ds(pl.multiple_of(core * (w_rows // 2), w_rows // 2), w_rows // 2)

    def columns_of(which, x_to):
        return pl.ds(pl.multiple_of((halves[which] * NX + x_to) * columns, columns), columns)

    fetches = [
        pltpu.make_async_copy(source, target, in_sem.at[number])
        for number, (source, target) in enumerate(
            (
                (basis_hbm, basis_ref), (nk_hbm, nk_ref), (pk_hbm, pk_ref), (nv_hbm, nv_ref),
                (pv_hbm, pv_ref), (q_hbm, q_ref),
                (w_hbm.at[:, columns_of(0, x)], w_ref.at[0, x]), (w_hbm.at[:, columns_of(1, x)], w_ref.at[1, x]),
            )
        )
    ]
    for fetch in fetches[:5]:
        fetch.start()

    barrier = pltpu.get_barrier_semaphore()
    friends = [at(z_to=z_peers[k]) for k in range(1, NZ)] + [at(x_to=x_peers[k]) for k in range(1, NX)]
    friends += [at(y_to=y_to[way]) for y_to in (y_next, y_after) for way in range(2)]
    friends += [at(core_to=1 - core), at(zh_to=1 - zh)]
    for friend in friends:
        pl.semaphore_signal(barrier, inc=1, device_id=friend, device_id_type=MESH)

    for fetch in fetches[5:]:
        fetch.start()
    diagonal[...] = jnp.zeros_like(diagonal)
    for fetch in fetches[:5]:
        fetch.wait()

    def z_copy(pair, k):
        return pltpu.make_async_remote_copy(
            src_ref=zsend.at[pair, pl.ds(0, 2)], dst_ref=kv.at[0, 0, k],
            send_sem=zs_sem.at[k], recv_sem=zr_sem.at[k], device_id=at(z_to=pair), device_id_type=MESH,
        )

    def send_pair(pair):
        @pl.when(z != pair)
        def _():
            z_copy(pair, lax.rem(pair - z + NZ, NZ)).start()

    rank = basis_ref.shape[2]
    for number in range(4):
        diagonal[number * rank : (number + 1) * rank, number * HD : (number + 1) * HD] = basis_ref[number // 2, number % 2]
    maps = diagonal[...]
    shared = jnp.concatenate([pk_ref[...], pv_ref[...]], axis=1)
    fresh = [jnp.concatenate([nk_ref[step], nv_ref[step]], axis=1) for step in range(2)]
    mapped = nt_dot(jnp.concatenate([*fresh, shared], axis=0), maps)
    shared_mapped = mapped[2 * rows :]
    for step in range(2):
        coefficients = (mapped[step * rows : (step + 1) * rows] - shared_mapped).astype(jnp.bfloat16)
        shared = (shared.astype(jnp.float32) + nn_dot(coefficients, maps)).astype(jnp.bfloat16)
        if step == 0:
            shared_mapped = nt_dot(shared, maps)
        for number in range(4):
            zsend[2 * (number % 2) + step, number // 2] = shared[:, number * HD : (number + 1) * HD]
        if step == 0:
            pl.semaphore_wait(barrier, len(friends))
        for head in range(2):
            send_pair(2 * head + step)

    started = []

    def send(src, dst, send_sem, recv_sem, device):
        copy = pltpu.make_async_remote_copy(
            src_ref=src, dst_ref=dst, send_sem=send_sem, recv_sem=recv_sem, device_id=device, device_id_type=MESH
        )
        copy.start()
        started.append(copy)
        return copy

    z_copies, q_copies = {}, {}
    for k in range(1, NZ):
        z_copies[k] = z_copy(z_peers[k], k)
        started.append(z_copies[k])
    kv[0, 0, 0] = zsend[z, 0:2]
    fetches[5].wait()
    for head in range(2):
        for step in range(2):
            zsend[2 * head + step, 2] = q_ref[step, :, head * HD : (head + 1) * HD]
    for k in range(1, NZ):
        q_copies[k] = send(zsend.at[z_peers[k], 2], qbuf.at[k], qs_sem.at[k], qr_sem.at[k], at(z_to=z_peers[k]))
    w_copies = {}
    for k in (2, 1, 3):
        for which in range(2):
            w_copies[k, which] = send(
                w_hbm.at[core_rows, columns_of(which, x_peers[k])], w_ref.at[which, x, core_rows],
                ws_sem.at[k, which], wr_sem.at[k, which], at(x_to=x_peers[k]),
            )
    qbuf[0] = zsend[z, 2]

    ring, share, far_other = {}, {}, {}

    def push(way, distance, chunk, step):
        piece = pl.ds(chunk * PER, PER)
        ring[way, distance + step, chunk] = send(
            kv.at[0, slot_of(way, distance), piece],
            kv.at[0, slot_of(way, distance + step), piece],
            rs_sem.at[way, distance + step - 1, chunk],
            rr_sem.at[way, distance + step - 1, chunk],
            at(y_to=(y_next if step == 1 else y_after)[way]),
        )

    def far_push(way, chunk):
        push(way, HALF - 2, chunk, 2)
        piece = pl.ds(chunk * PER, PER)
        far_other[chunk] = send(
            kv.at[0, slot_of(way, HALF - 2), piece], kv.at[1, slot_of(0, HALF), piece],
            fs_sem.at[chunk], fr_sem.at[chunk], at(y_to=y_after[way], core_to=1 - core),
        )

    def share_core(way, distance, chunk):
        parts = 1 if distance < HALF - 1 else 2
        count = CHUNKS // parts
        if (chunk + 1) % count:
            return
        part = chunk // count
        piece = pl.ds(part * count * PER, count * PER)
        slot = slot_of(way, distance)
        share[slot, part] = send(
            kv.at[0, slot, piece],
            kv.at[1, slot, piece],
            cs_sem.at[slot, part],
            cr_sem.at[slot, part],
            at(core_to=1 - core),
        )

    lag = 2
    for chunk in range(CHUNKS + lag):
        if chunk < CHUNKS:
            for k in range(chunk * PER, (chunk + 1) * PER):
                if k:
                    z_copies[k].wait_recv()
            for way in range(2):
                push(way, 0, chunk, 2)
            share_core(0, 0, chunk)
        if chunk >= lag:
            for way in range(2):
                push(way, 0, chunk - lag, 1)
    scale = HD ** (-0.5)
    block = NZ * rows
    lane_max = {}

    def group_of(distance):
        return int(distance >= HALF - 1)

    def score(side, distance):
        first, last = slot_of(0, distance), slot_of(1, distance)
        count = last - first + 1
        keys = kv[side, first : last + 1, :, 0].reshape(count * block, HD)
        begin = (side * NY + first) * block
        found = nt_dot(queries, keys) * scale
        scores[:, begin : begin + count * block] = found
        for number in range(count):
            piece = found[:, number * block : (number + 1) * block]
            group = group_of(distance)
            lane_max[group] = jnp.maximum(lane_max[group], piece) if group in lane_max else piece

    def score_other(distance):
        for slot in sorted({slot_of(0, distance), slot_of(1, distance)}):
            for part in range(2):
                if (slot, part) in share:
                    share[slot, part].wait_recv()
        for chunk in range(CHUNKS if distance == HALF else 0):
            far_other[chunk].wait_recv()
        score(1, distance)

    for chunk in range(CHUNKS):
        for way in range(2):
            ring[way, HALF - 2, chunk].wait_recv()
            push(way, HALF - 2, chunk, 1)
        far_push(far_way(chunk), chunk)
        for way in range(2):
            share_core(way, HALF - 2, chunk)
    for k in range(1, NZ):
        q_copies[k].wait_recv()
    queries = qbuf[...].reshape(NZ * rows, HD)
    score(0, 0)
    for chunk in range(CHUNKS):
        for way in range(2):
            ring[way, 1, chunk].wait_recv()
            share_core(way, 1, chunk)
    score(0, 2)
    score(0, 1)
    score_other(0)
    def weigh(group, row_max, own_rows):
        slots = [slot_of(way, distance) for distance in range(HALF + 1) for way in range(2) if group_of(distance) == group]
        first, last = min(slots), max(slots)
        count = last - first + 1
        lane_total = jnp.zeros((row_max.shape[0], block), jnp.float32)
        summed = jnp.zeros((row_max.shape[0], HD), jnp.float32)
        for side in range(2):
            begin = (side * NY + first) * block
            for number in range(count):
                span = slice(begin + number * block, begin + (number + 1) * block)
                exponent = jnp.exp(scores[own_rows, span] - row_max)
                lane_total = lane_total + exponent
                weights[own_rows, span] = exponent.astype(jnp.bfloat16)
            values = kv[side, first : last + 1, :, 1].reshape(count * block, HD)
            summed = summed + nn_dot(weights[own_rows, begin : begin + count * block], values)
        return lane_total, summed

    def share_last():
        for chunk in range(CHUNKS):
            for way in range(2):
                ring[way, HALF - 1, chunk].wait_recv()
                share_core(way, HALF - 1, chunk)

    score_other(2)
    score_other(1)
    near_max = jnp.max(lane_max[0], axis=1, keepdims=True)
    near_total, near_summed = weigh(0, near_max, slice(0, block))
    share_last()
    score(0, HALF - 1)
    for chunk in range(CHUNKS):
        ring[far_way(chunk), HALF, chunk].wait_recv()
    score(0, HALF)
    score_other(HALF)
    score_other(HALF - 1)

    earlier = list(started)
    a_copies = {}
    part, owners = block // 2, NZ // 2
    all_max = jnp.maximum(near_max, jnp.max(lane_max[1], axis=1, keepdims=True))
    for half in (1, 0):
        own_rows = slice(half * part, (half + 1) * part)
        rescale = jnp.exp(near_max[own_rows] - all_max[own_rows])
        far_total, far_summed = weigh(1, all_max[own_rows], own_rows)
        row_total = jnp.sum(near_total[own_rows] * rescale + far_total, axis=1, keepdims=True)
        attended = ((near_summed[own_rows] * rescale + far_summed) / row_total).astype(jnp.bfloat16)
        asend[half * owners : (half + 1) * owners] = attended.reshape(owners, rows, HD)
        for j in (2, 1, 3, 0):
            for k in range(half * owners, (half + 1) * owners):
                if k or j:
                    a_copies[k, j] = send(
                        asend.at[k], abuf.at[x, z], as_sem.at[k, j], ar_sem.at[k, j], at(z_to=z_back[k], x_to=x_peers[j])
                    )
    abuf[x, z] = asend[0]

    v_copies = {}
    for which in range(2):
        for k in (1, 3, 2):
            w_copies[k, which].wait_recv()
            there = w_ref.at[which, x_back[k], core_rows]
            v_copies[k, which] = send(there, there, vs_sem.at[k, which], vr_sem.at[k, which], at(core_to=1 - core))
    for fetch in fetches[6:]:
        fetch.wait()
    for copy in earlier:
        copy.wait_send()
    for copy in a_copies.values():
        copy.wait_recv()
    by_step = [
        jnp.concatenate([abuf[j, 2 * head + step] for j in range(NX) for head in range(2)], axis=1) for step in range(2)
    ]
    features = jnp.concatenate(by_step, axis=0)

    def partial(which):
        for k in range(1, NX):
            v_copies[k, which].wait_recv()
        found = nn_dot(features, w_ref[which].reshape(NX * w_rows, columns))
        return found.reshape(2, rows, columns)

    there = partial(0)
    hsend[...] = there.astype(jnp.bfloat16)
    h_copies = []
    for step in range(2):
        h_copies.append(send(hsend.at[step], hrecv.at[step], hs_sem.at[step], hr_sem.at[step], at(zh_to=1 - zh)))
    here = partial(1)
    for copy in [*a_copies.values(), *v_copies.values()]:
        copy.wait_send()
    for step in range(2):
        h_copies[step].wait_recv()
        out_ref[step] = here[step] + hrecv[step].astype(jnp.float32)
    for copy in h_copies:
        copy.wait_send()


def per_device(queries, new_keys, new_values, prev_keys, prev_values, kv_basis, out_weight, out_gate):
    steps, rows, _ = queries.shape
    columns = out_gate.shape[1]
    bf16, f32 = jnp.bfloat16, jnp.float32
    vmem = pl.BlockSpec(memory_space=pltpu.VMEM)
    dma = pltpu.SemaphoreType.DMA
    tokens = 2 * NY * NZ * rows
    operands = (
        queries, new_keys, new_values, prev_keys, prev_values, jnp.swapaxes(kv_basis, 2, 3), out_weight,
    )
    summed = pl.pallas_call(
        kernel,
        out_shape=jax.ShapeDtypeStruct((steps, rows, columns), f32),
        in_specs=[pl.BlockSpec(memory_space=pltpu.HBM)] * 7,
        out_specs=vmem,
        scratch_shapes=[
            *[pltpu.VMEM(operand.shape, bf16) for operand in operands[:6]],
            pltpu.VMEM((2, NX, out_weight.shape[0], columns), bf16),
            pltpu.VMEM((4 * kv_basis.shape[3], 4 * HD), bf16),
            pltpu.VMEM((NZ, 3, rows, HD), bf16),
            pltpu.VMEM((2, NY, NZ, 2, rows, HD), bf16),
            pltpu.VMEM((NZ, rows, HD), bf16),
            pltpu.VMEM((NZ * rows, tokens), f32),
            pltpu.VMEM((NZ * rows, tokens), bf16),
            pltpu.VMEM((NZ, rows, HD), bf16),
            pltpu.VMEM((NX, NZ, rows, HD), bf16),
            pltpu.VMEM((steps, rows, columns), bf16),
            pltpu.VMEM((steps, rows, columns), bf16),
            dma((8,)),
            dma((NZ,)), dma((NZ,)), dma((NZ,)), dma((NZ,)),
            dma((2, HALF, CHUNKS)), dma((2, HALF, CHUNKS)),
            dma((NY, 2)), dma((NY, 2)),
            dma((CHUNKS,)), dma((CHUNKS,)),
            dma((NZ, NX)), dma((NZ, NX)),
            dma((NX, 2)), dma((NX, 2)), dma((NX, 2)), dma((NX, 2)),
            dma((2,)), dma((2,)),
        ],
        compiler_params=pltpu.CompilerParams(
            collective_id=0, has_side_effects=True, vmem_limit_bytes=32 * 1024 * 1024
        ),
    )(*[pltpu.with_memory_space_constraint(operand, pltpu.HBM) for operand in operands])
    return (out_gate[:, None, :] * summed).astype(bf16)


def solution(mesh):
    placed = (
        P(None, "patch", "tp"),
        P(None, "patch", "tp"),
        P(None, "patch", "tp"),
        P("patch", "tp"),
        P("patch", "tp"),
        P(None, "tp", None, None),
        P("tp", None),
        P(None, "tp"),
    )
    return jax.shard_map(
        per_device, mesh=mesh, in_specs=placed, out_specs=P(None, "patch", "tp"), check_vma=False
    )
```

```python
import functools

import jax
import jax.numpy as jnp
from jax import lax
from jax.experimental import pallas as pl
from jax.experimental.pallas import tpu as pltpu
from jax.sharding import PartitionSpec as P

MESH = pl.DeviceIdType.MESH
NZ = 4
NY = 8
NX = 4
HD = 128
CHUNKS = 2
PER = NZ // CHUNKS
HALF = NY // 2


def slot_of(way, distance):
    if distance == 0 or distance == HALF:
        return 2 * distance - (distance == HALF)
    return 2 * distance - 1 + way


def far_way(chunk):
    return 0 if chunk < CHUNKS // 2 else 1


def nt_dot(a, b):
    return lax.dot_general(a, b, (((1,), (1,)), ((), ())), preferred_element_type=jnp.float32)


def nn_dot(a, b):
    return jnp.dot(a, b, preferred_element_type=jnp.float32)


def kernel(
    q_hbm, nk_hbm, nv_hbm, pk_hbm, pv_hbm, basis_hbm, w_hbm, out_ref,
    q_ref, nk_ref, nv_ref, pk_ref, pv_ref, basis_ref, w_ref,
    diagonal, zsend, kv, qbuf, scores, weights, asend, abuf, hsend, hrecv,
    in_sem, zs_sem, zr_sem, qs_sem, qr_sem, rs_sem, rr_sem, cs_sem, cr_sem,
    fs_sem, fr_sem, as_sem, ar_sem, ws_sem, wr_sem, vs_sem, vr_sem, hs_sem, hr_sem,
):
    rows = pk_ref.shape[0]
    columns = out_ref.shape[2]
    patch, tp = lax.axis_index("patch"), lax.axis_index("tp")
    core = patch % 2
    y = (patch // 2) % NY
    z = patch // (2 * NY)
    x = tp % NX
    zh = tp // NX

    def at(z_to=None, y_to=None, core_to=None, x_to=None, zh_to=None):
        z_t = z if z_to is None else z_to
        y_t = y if y_to is None else y_to
        c_t = core if core_to is None else core_to
        x_t = x if x_to is None else x_to
        h_t = zh if zh_to is None else zh_to
        return ((z_t * NY + y_t) * 2 + c_t, h_t * NX + x_t)

    z_peers = [lax.rem(z + k, NZ) for k in range(NZ)]
    z_back = [lax.rem(z + NZ - k, NZ) for k in range(NZ)]
    x_peers = [lax.rem(x + k, NX) for k in range(NX)]
    x_back = [lax.rem(x + NX - k, NX) for k in range(NX)]
    y_next = [lax.rem(y + 1, NY), lax.rem(y + NY - 1, NY)]
    y_after = [lax.rem(y + 2, NY), lax.rem(y + NY - 2, NY)]

    halves = (1 - zh, zh)
    w_rows = w_hbm.shape[0]
    core_rows = pl.ds(pl.multiple_of(core * (w_rows // 2), w_rows // 2), w_rows // 2)

    def columns_of(which, x_to):
        return pl.ds(pl.multiple_of((halves[which] * NX + x_to) * columns, columns), columns)

    fetches = [
        pltpu.make_async_copy(source, target, in_sem.at[number])
        for number, (source, target) in enumerate(
            (
                (basis_hbm, basis_ref), (nk_hbm, nk_ref), (pk_hbm, pk_ref), (nv_hbm, nv_ref),
                (pv_hbm, pv_ref), (q_hbm, q_ref),
                (w_hbm.at[:, columns_of(0, x)], w_ref.at[0, x]), (w_hbm.at[:, columns_of(1, x)], w_ref.at[1, x]),
            )
        )
    ]
    for fetch in fetches[:5]:
        fetch.start()

    barrier = pltpu.get_barrier_semaphore()
    friends = [at(z_to=z_peers[k]) for k in range(1, NZ)] + [at(x_to=x_peers[k]) for k in range(1, NX)]
    friends += [at(y_to=y_to[way]) for y_to in (y_next, y_after) for way in range(2)]
    friends += [at(core_to=1 - core), at(zh_to=1 - zh)]
    for friend in friends:
        pl.semaphore_signal(barrier, inc=1, device_id=friend, device_id_type=MESH)

    for fetch in fetches[5:]:
        fetch.start()
    diagonal[...] = jnp.zeros_like(diagonal)
    for fetch in fetches[:5]:
        fetch.wait()

    def z_copy(pair, k):
        return pltpu.make_async_remote_copy(
            src_ref=zsend.at[pair, pl.ds(0, 2)], dst_ref=kv.at[0, 0, k],
            send_sem=zs_sem.at[k], recv_sem=zr_sem.at[k], device_id=at(z_to=pair), device_id_type=MESH,
        )

    def send_pair(pair):
        @pl.when(z != pair)
        def _():
            z_copy(pair, lax.rem(pair - z + NZ, NZ)).start()

    rank = basis_ref.shape[2]
    for number in range(4):
        diagonal[number * rank : (number + 1) * rank, number * HD : (number + 1) * HD] = basis_ref[number // 2, number % 2]
    maps = diagonal[...]
    shared = jnp.concatenate([pk_ref[...], pv_ref[...]], axis=1)
    fresh = [jnp.concatenate([nk_ref[step], nv_ref[step]], axis=1) for step in range(2)]
    mapped = nt_dot(jnp.concatenate([*fresh, shared], axis=0), maps)
    shared_mapped = mapped[2 * rows :]
    for step in range(2):
        coefficients = (mapped[step * rows : (step + 1) * rows] - shared_mapped).astype(jnp.bfloat16)
        shared = (shared.astype(jnp.float32) + nn_dot(coefficients, maps)).astype(jnp.bfloat16)
        if step == 0:
            shared_mapped = nt_dot(shared, maps)
        for number in range(4):
            zsend[2 * (number % 2) + step, number // 2] = shared[:, number * HD : (number + 1) * HD]
        if step == 0:
            pl.semaphore_wait(barrier, len(friends))
        for head in range(2):
            send_pair(2 * head + step)

    started = []

    def send(src, dst, send_sem, recv_sem, device):
        copy = pltpu.make_async_remote_copy(
            src_ref=src, dst_ref=dst, send_sem=send_sem, recv_sem=recv_sem, device_id=device, device_id_type=MESH
        )
        copy.start()
        started.append(copy)
        return copy

    z_copies, q_copies = {}, {}
    for k in range(1, NZ):
        z_copies[k] = z_copy(z_peers[k], k)
        started.append(z_copies[k])
    kv[0, 0, 0] = zsend[z, 0:2]
    fetches[5].wait()
    for head in range(2):
        for step in range(2):
            zsend[2 * head + step, 2] = q_ref[step, :, head * HD : (head + 1) * HD]
    w_copies = {}
    for k in (2, 1, 3):
        for which in range(2):
            w_copies[k, which] = send(
                w_hbm.at[core_rows, columns_of(which, x_peers[k])], w_ref.at[which, x, core_rows],
                ws_sem.at[k, which], wr_sem.at[k, which], at(x_to=x_peers[k]),
            )
    qbuf[0] = zsend[z, 2]

    ring, share, far_other = {}, {}, {}

    def push(way, distance, chunk, step):
        piece = pl.ds(chunk * PER, PER)
        ring[way, distance + step, chunk] = send(
            kv.at[0, slot_of(way, distance), piece],
            kv.at[0, slot_of(way, distance + step), piece],
            rs_sem.at[way, distance + step - 1, chunk],
            rr_sem.at[way, distance + step - 1, chunk],
            at(y_to=(y_next if step == 1 else y_after)[way]),
        )

    def far_push(way, chunk):
        push(way, HALF - 2, chunk, 2)
        piece = pl.ds(chunk * PER, PER)
        far_other[chunk] = send(
            kv.at[0, slot_of(way, HALF - 2), piece], kv.at[1, slot_of(0, HALF), piece],
            fs_sem.at[chunk], fr_sem.at[chunk], at(y_to=y_after[way], core_to=1 - core),
        )

    def share_core(way, distance, chunk):
        parts = 1 if distance < HALF - 1 else 2
        count = CHUNKS // parts
        if (chunk + 1) % count:
            return
        part = chunk // count
        piece = pl.ds(part * count * PER, count * PER)
        slot = slot_of(way, distance)
        share[slot, part] = send(
            kv.at[0, slot, piece],
            kv.at[1, slot, piece],
            cs_sem.at[slot, part],
            cr_sem.at[slot, part],
            at(core_to=1 - core),
        )

    lag = 2
    for chunk in range(CHUNKS + lag):
        if chunk < CHUNKS:
            for k in range(chunk * PER, (chunk + 1) * PER):
                if k:
                    z_copies[k].wait_recv()
            for way in range(2):
                push(way, 0, chunk, 2)
            share_core(0, 0, chunk)
        if chunk >= lag:
            for way in range(2):
                push(way, 0, chunk - lag, 1)
        if chunk == 0:
            for k in range(1, NZ):
                q_copies[k] = send(
                    zsend.at[z_peers[k], 2], qbuf.at[k], qs_sem.at[k], qr_sem.at[k], at(z_to=z_peers[k])
                )
    for k in range(1, NZ):
        q_copies[k].wait_recv()
    queries = qbuf[...].reshape(NZ * rows, HD)
    scale = HD ** (-0.5)
    block = NZ * rows
    lane_max = {}

    def group_of(distance):
        return int(distance >= HALF - 1)

    def score(side, distance):
        first, last = slot_of(0, distance), slot_of(1, distance)
        count = last - first + 1
        keys = kv[side, first : last + 1, :, 0].reshape(count * block, HD)
        begin = (side * NY + first) * block
        found = nt_dot(queries, keys) * scale
        scores[:, begin : begin + count * block] = found
        for number in range(count):
            piece = found[:, number * block : (number + 1) * block]
            group = group_of(distance)
            lane_max[group] = jnp.maximum(lane_max[group], piece) if group in lane_max else piece

    def score_other(distance):
        for slot in sorted({slot_of(0, distance), slot_of(1, distance)}):
            for part in range(2):
                if (slot, part) in share:
                    share[slot, part].wait_recv()
        for chunk in range(CHUNKS if distance == HALF else 0):
            far_other[chunk].wait_recv()
        score(1, distance)

    score(0, 0)
    for chunk in range(CHUNKS):
        for way in range(2):
            ring[way, HALF - 2, chunk].wait_recv()
            push(way, HALF - 2, chunk, 1)
        far_push(far_way(chunk), chunk)
        for way in range(2):
            share_core(way, HALF - 2, chunk)
    for chunk in range(CHUNKS):
        for way in range(2):
            ring[way, 1, chunk].wait_recv()
            share_core(way, 1, chunk)
    score(0, 2)
    score(0, 1)
    score_other(0)
    def weigh(group, row_max, own_rows):
        slots = [slot_of(way, distance) for distance in range(HALF + 1) for way in range(2) if group_of(distance) == group]
        first, last = min(slots), max(slots)
        count = last - first + 1
        lane_total = jnp.zeros((row_max.shape[0], block), jnp.float32)
        summed = jnp.zeros((row_max.shape[0], HD), jnp.float32)
        for side in range(2):
            begin = (side * NY + first) * block
            for number in range(count):
                span = slice(begin + number * block, begin + (number + 1) * block)
                exponent = jnp.exp(scores[own_rows, span] - row_max)
                lane_total = lane_total + exponent
                weights[own_rows, span] = exponent.astype(jnp.bfloat16)
            values = kv[side, first : last + 1, :, 1].reshape(count * block, HD)
            summed = summed + nn_dot(weights[own_rows, begin : begin + count * block], values)
        return lane_total, summed

    def share_last():
        for chunk in range(CHUNKS):
            for way in range(2):
                ring[way, HALF - 1, chunk].wait_recv()
                share_core(way, HALF - 1, chunk)

    score_other(2)
    score_other(1)
    near_max = jnp.max(lane_max[0], axis=1, keepdims=True)
    near_total, near_summed = weigh(0, near_max, slice(0, block))
    share_last()
    score(0, HALF - 1)
    for chunk in range(CHUNKS):
        ring[far_way(chunk), HALF, chunk].wait_recv()
    score(0, HALF)
    score_other(HALF)
    score_other(HALF - 1)

    earlier = list(started)
    a_copies = {}
    part, owners = block // 2, NZ // 2
    all_max = jnp.maximum(near_max, jnp.max(lane_max[1], axis=1, keepdims=True))
    for half in (1, 0):
        own_rows = slice(half * part, (half + 1) * part)
        rescale = jnp.exp(near_max[own_rows] - all_max[own_rows])
        far_total, far_summed = weigh(1, all_max[own_rows], own_rows)
        row_total = jnp.sum(near_total[own_rows] * rescale + far_total, axis=1, keepdims=True)
        attended = ((near_summed[own_rows] * rescale + far_summed) / row_total).astype(jnp.bfloat16)
        asend[half * owners : (half + 1) * owners] = attended.reshape(owners, rows, HD)
        for j in (2, 1, 3, 0):
            for k in range(half * owners, (half + 1) * owners):
                if k or j:
                    a_copies[k, j] = send(
                        asend.at[k], abuf.at[x, z], as_sem.at[k, j], ar_sem.at[k, j], at(z_to=z_back[k], x_to=x_peers[j])
                    )
    abuf[x, z] = asend[0]

    v_copies = {}
    for which in range(2):
        for k in (1, 3, 2):
            w_copies[k, which].wait_recv()
            there = w_ref.at[which, x_back[k], core_rows]
            v_copies[k, which] = send(there, there, vs_sem.at[k, which], vr_sem.at[k, which], at(core_to=1 - core))
    for fetch in fetches[6:]:
        fetch.wait()
    for copy in a_copies.values():
        copy.wait_recv()
    by_step = [
        jnp.concatenate([abuf[j, 2 * head + step] for j in range(NX) for head in range(2)], axis=1) for step in range(2)
    ]
    features = jnp.concatenate(by_step, axis=0)

    def partial(which):
        for k in range(1, NX):
            v_copies[k, which].wait_recv()
        found = nn_dot(features, w_ref[which].reshape(NX * w_rows, columns))
        return found.reshape(2, rows, columns)

    there = partial(0)
    hsend[...] = there.astype(jnp.bfloat16)
    h_copies = []
    for step in range(2):
        h_copies.append(send(hsend.at[step], hrecv.at[step], hs_sem.at[step], hr_sem.at[step], at(zh_to=1 - zh)))
    here = partial(1)
    for copy in earlier:
        copy.wait_send()
    for copy in [*a_copies.values(), *v_copies.values()]:
        copy.wait_send()
    for step in range(2):
        h_copies[step].wait_recv()
        out_ref[step] = here[step] + hrecv[step].astype(jnp.float32)
    for copy in h_copies:
        copy.wait_send()


def per_device(queries, new_keys, new_values, prev_keys, prev_values, kv_basis, out_weight, out_gate):
    steps, rows, _ = queries.shape
    columns = out_gate.shape[1]
    bf16, f32 = jnp.bfloat16, jnp.float32
    vmem = pl.BlockSpec(memory_space=pltpu.VMEM)
    dma = pltpu.SemaphoreType.DMA
    tokens = 2 * NY * NZ * rows
    operands = (
        queries, new_keys, new_values, prev_keys, prev_values, jnp.swapaxes(kv_basis, 2, 3), out_weight,
    )
    summed = pl.pallas_call(
        kernel,
        out_shape=jax.ShapeDtypeStruct((steps, rows, columns), f32),
        in_specs=[pl.BlockSpec(memory_space=pltpu.HBM)] * 7,
        out_specs=vmem,
        scratch_shapes=[
            *[pltpu.VMEM(operand.shape, bf16) for operand in operands[:6]],
            pltpu.VMEM((2, NX, out_weight.shape[0], columns), bf16),
            pltpu.VMEM((4 * kv_basis.shape[3], 4 * HD), bf16),
            pltpu.VMEM((NZ, 3, rows, HD), bf16),
            pltpu.VMEM((2, NY, NZ, 2, rows, HD), bf16),
            pltpu.VMEM((NZ, rows, HD), bf16),
            pltpu.VMEM((NZ * rows, tokens), f32),
            pltpu.VMEM((NZ * rows, tokens), bf16),
            pltpu.VMEM((NZ, rows, HD), bf16),
            pltpu.VMEM((NX, NZ, rows, HD), bf16),
            pltpu.VMEM((steps, rows, columns), bf16),
            pltpu.VMEM((steps, rows, columns), bf16),
            dma((8,)),
            dma((NZ,)), dma((NZ,)), dma((NZ,)), dma((NZ,)),
            dma((2, HALF, CHUNKS)), dma((2, HALF, CHUNKS)),
            dma((NY, 2)), dma((NY, 2)),
            dma((CHUNKS,)), dma((CHUNKS,)),
            dma((NZ, NX)), dma((NZ, NX)),
            dma((NX, 2)), dma((NX, 2)), dma((NX, 2)), dma((NX, 2)),
            dma((2,)), dma((2,)),
        ],
        compiler_params=pltpu.CompilerParams(
            collective_id=0, has_side_effects=True, vmem_limit_bytes=32 * 1024 * 1024
        ),
    )(*[pltpu.with_memory_space_constraint(operand, pltpu.HBM) for operand in operands])
    return (out_gate[:, None, :] * summed).astype(bf16)


def solution(mesh):
    placed = (
        P(None, "patch", "tp"),
        P(None, "patch", "tp"),
        P(None, "patch", "tp"),
        P("patch", "tp"),
        P("patch", "tp"),
        P(None, "tp", None, None),
        P("tp", None),
        P(None, "tp"),
    )
    return jax.shard_map(
        per_device, mesh=mesh, in_specs=placed, out_specs=P(None, "patch", "tp"), check_vma=False
    )
```
